256 devices in a mesh: row: 32 (over x, z), col: 8 (over y, core).
Axes of the slice: x: 4, y: 4, z: 8, core: 2. Of those that a mesh axis runs over, the one named last changes fastest.
Arguments:
- spectrum: float32 [2, 8192, 8192], P(None, 'row', 'col'), may hold values from -6 to 6
- pupil: float32 [2, 512, 512], replicated, may hold values from -4.2 to 4.2
- amplitude: float32 [32, 8, 512, 512], P('row', 'col'), may hold values from 0 to 4, as said below
- offsets: int32 [32, 8, 2], P('row', 'col'), may hold values from 0 to 7680, as said below
- holds: int32 [32, 8], P('row', 'col'), may hold values from 0 to 1, as said below
Outputs:
- spectrum_grad: float32 [2, 8192, 8192], P(None, 'row', 'col')
- transposed_image: float32 [2, 8192, 8192], P(None, ('row', 'col'))
The draws below stay inside these ranges and needn't reach their ends.
Inputs may be any that keep to these rules, and one draw needn't show every extreme that they name: In each pair of devices in one col whose row indices differ only in the lowest bit, exactly one has holds 1; 128 LEDs in all. `offsets`: both rows of a pair carry the corner (oy, ox) of that pair's LED. With h the row index of the holding device and c the col index: h * 256 - 256 <= oy <= h * 256 + 256, both ends reached by some LED in every draw; c * 1024 <= ox <= c * 1024 + 512, both ends reached by some LED in every draw. `amplitude`: zero on devices whose holds is 0, positive elsewhere.
All inputs are finite; a program needn't handle non-finite values.
Results may differ from the reference program's by a relative error of at most 0.00011.
Values sent between devices are 32-bit elements; how exact they have to be, the bound alone decides.
No kernel may reach another device: no remote copies, remote signals or barrier semaphores. Data moves between devices by JAX's collectives and lax.ppermute only.
A program may use at most 128 MiB of HBM per device.

```python
import jax
import jax.numpy as jnp
from jax import lax

N = 8192
M = 512
BLOCK_ROWS = 256
BLOCK_COLS = 1024
N_ROW = 32
N_COL = 8


def pair_choice(key):
    return jax.random.randint(key, (N_ROW // 2, N_COL), 0, 2)


def device_flags(choose_bits):
    even_rows = 1 - choose_bits
    return jnp.stack([even_rows, choose_bits], axis=1).reshape(N_ROW, N_COL)


def draw_holds(key, part):
    choose_bits = pair_choice(key)
    return device_flags(choose_bits).astype(jnp.int32)


def draw_offsets(key, part):
    choose_bits = pair_choice(key)
    key = jax.random.fold_in(key, 5)
    pair_row = jnp.arange(N_ROW // 2, dtype=jnp.int32)[:, None]
    col_index = jnp.arange(N_COL, dtype=jnp.int32)[None, :]
    holder_row = 2 * pair_row + choose_bits
    shift_rows = jax.random.randint(jax.random.fold_in(key, 1), (N_ROW // 2, N_COL), -BLOCK_ROWS, BLOCK_ROWS + 1)
    shift_cols = jax.random.randint(jax.random.fold_in(key, 2), (N_ROW // 2, N_COL), 0, BLOCK_COLS - M + 1)
    first_pair = jnp.logical_and(pair_row == 0, col_index == 0)
    second_pair = jnp.logical_and(pair_row == 1, col_index == 0)
    shift_rows = jnp.where(first_pair, BLOCK_ROWS, jnp.where(second_pair, -BLOCK_ROWS, shift_rows))
    shift_cols = jnp.where(first_pair, BLOCK_COLS - M, jnp.where(second_pair, 0, shift_cols))
    corner_row = jnp.clip(holder_row * BLOCK_ROWS + shift_rows, 0, N - M)
    corner_col = col_index * BLOCK_COLS + shift_cols
    pair_corner = jnp.stack([corner_row, corner_col], axis=-1)
    return jnp.repeat(pair_corner, 2, axis=0).astype(jnp.int32)


def draw_amplitude(key, part):
    choose_bits = pair_choice(key)
    key = jax.random.fold_in(key, 7)
    flags = device_flags(choose_bits).astype(jnp.float32)
    values = jnp.exp(jax.random.uniform(key, (N_ROW, N_COL, M, M), jnp.float32, jnp.log(0.5), jnp.log(3.0)))
    return values * flags[:, :, None, None]


def levels(key, extent, cuts, least, high):
    factor_of = 1.0
    for axis_at, parts in cuts:
        heights = jax.random.uniform(jax.random.fold_in(jax.random.fold_in(key, 6), axis_at), (parts,), jnp.float32, least / len(cuts), high / len(cuts))
        factor_of = factor_of * jnp.repeat(jnp.exp(heights), extent[axis_at] // parts).reshape((-1,) + (1,) * (len(extent) - 1 - axis_at))
    return factor_of


def scatter_about(key, shape, spread, reach, shards=(), kind=jnp.bfloat16):
    array = jax.random.normal(key, shape, jnp.float32) * spread
    if len(shards) > 0:
        array = levels(key, shape, shards, -0.22, 0.18) * array
    return jnp.clip(array, min=-reach, max=reach).astype(kind)


def setup_inputs(seed: int = 0) -> dict:
    keys = jax.random.split(jax.random.key(seed), 6)
    spectrum = scatter_about(keys[0], (2, N, N), 1.0, 6.0, ((1, 32), (2, 8)), jnp.float32)
    pupil = scatter_about(keys[1], (2, M, M), 0.7, 4.2, (), jnp.float32)
    amplitude = draw_amplitude(jax.random.fold_in(keys[5], 71), 0)
    offsets = draw_offsets(jax.random.fold_in(keys[5], 71), 0)
    holds = draw_holds(jax.random.fold_in(keys[5], 71), 0)
    return {"spectrum": spectrum, "pupil": pupil, "amplitude": amplitude, "offsets": offsets, "holds": holds}


GAMMA = 1.0

def reference(spectrum, pupil, amplitude, offsets, holds):
    spec_full = spectrum[0] + 1j * spectrum[1]
    lens_full = pupil[0] + 1j * pupil[1]
    slot_count = N_ROW * N_COL
    flat_measured = amplitude.reshape(slot_count, M, M)
    flat_offsets = offsets.reshape(slot_count, 2).astype(jnp.int32)
    flat_holds = holds.reshape(slot_count).astype(spectrum.dtype)

    def add_window(running, slot_data):
        measured, corner, weight = slot_data
        window = lax.dynamic_slice(spec_full, (corner[0], corner[1]), (M, M))
        wave_field = jnp.fft.ifft2(lens_full * window, norm='ortho')
        modulus = jnp.sqrt(wave_field.real * wave_field.real + wave_field.imag * wave_field.imag + GAMMA)
        fitted = wave_field * (1.0 - measured / modulus)
        update = jnp.conj(lens_full) * jnp.fft.fft2(fitted, norm='ortho') * weight
        current = lax.dynamic_slice(running, (corner[0], corner[1]), (M, M))
        return (lax.dynamic_update_slice(running, current + update, (corner[0], corner[1])), None)
    running, trailing = lax.scan(add_window, jnp.zeros_like(spec_full), (flat_measured, flat_offsets, flat_holds))
    image_full = jnp.fft.ifft2(running, norm='ortho').T
    spectrum_grad = jnp.stack([running.real, running.imag]).astype(jnp.float32)
    transposed_image = jnp.stack([image_full.real, image_full.imag]).astype(jnp.float32)
    return (spectrum_grad, transposed_image)
```

```python
import math

import jax
import jax.numpy as jnp
import ml_dtypes
import numpy as np
from jax import lax
from jax.experimental import pallas as pl
from jax.experimental.pallas import tpu as pltpu
from jax.sharding import PartitionSpec as P

GAMMA = 1.0
N = 8192
M = 512
ROWS = 256
COLS = 1024
N_ROW = 32
N_COL = 8
PARTS = N_ROW * N_COL
LOW = 32
F32 = jnp.float32
BF16 = jnp.bfloat16
VMEM_BYTES = 32 * 1024 * 1024


def halves(table):
    high = table.astype(np.float32).astype(ml_dtypes.bfloat16)
    low = (table - high.astype(np.float64)).astype(np.float32).astype(ml_dtypes.bfloat16)
    return high, low


def dft_tables(length, scale):
    counter = np.arange(length)
    angles = 2.0 * np.pi / length * (np.outer(counter, counter) % length)
    return np.stack(halves(np.cos(angles) * scale) + halves(np.sin(angles) * scale))


def twist_tables():
    angles = 2.0 * np.pi / N * np.outer(np.arange(LOW), np.arange(PARTS))
    return np.stack([np.cos(angles), np.sin(angles)]).astype(np.float32)


def split(values):
    high = values.astype(BF16)
    low = (values - high.astype(F32)).astype(BF16)
    return high, low


def mm(left, right):
    return jnp.dot(left, right, preferred_element_type=F32)


def mm3(left, right):
    return mm(left[0], right[0]) + mm(left[0], right[1]) + mm(left[1], right[0])


def complex_times_table(re, im, cos, sin, sign):
    rc, rs, ic, is_ = mm3(re, cos), mm3(re, sin), mm3(im, cos), mm3(im, sin)
    if sign > 0:
        return rc - is_, rs + ic
    return rc + is_, ic - rs


def table_times_complex(cos, sin, sign, re, im):
    rc, rs, ic, is_ = mm3(cos, re), mm3(sin, re), mm3(cos, im), mm3(sin, im)
    if sign > 0:
        return rc - is_, rs + ic
    return rc + is_, ic - rs


def turn(value, numer, denom):
    re, im = value
    numer %= denom
    if numer == 0:
        return re, im
    if 4 * numer == denom:
        return -im, re
    if 2 * numer == denom:
        return -re, -im
    cos = math.cos(2.0 * math.pi * numer / denom)
    sin = math.sin(2.0 * math.pi * numer / denom)
    if 8 * numer == denom:
        return (re - im) * cos, (re + im) * cos
    if 8 * numer == 3 * denom:
        return (re + im) * -sin, (re - im) * sin
    return re * cos - im * sin, re * sin + im * cos


def fft_list(values):
    count = len(values)
    if count == 1:
        return values
    even = fft_list(values[0::2])
    odd = fft_list(values[1::2])
    first, second = [], []
    for at in range(count // 2):
        er, ei = even[at]
        tr, ti = turn(odd[at], at, count)
        first.append((er + tr, ei + ti))
        second.append((er - tr, ei - ti))
    return first + second


def window_rows(base, corner, shape):
    rows = lax.broadcasted_iota(jnp.int32, shape, 0) + base
    return rows, rows < corner, rows >= corner + M


def call(kernel, outs, smem, *args):
    specs = [pl.BlockSpec(memory_space=pltpu.SMEM if at in smem else pltpu.VMEM) for at in range(len(args))]
    return lambda scratch=(): pl.pallas_call(
        kernel,
        out_shape=tuple(jax.ShapeDtypeStruct(shape, F32) for shape in outs),
        in_specs=specs,
        out_specs=tuple(pl.BlockSpec(memory_space=pltpu.VMEM) for _ in outs),
        scratch_shapes=scratch,
        compiler_params=pltpu.CompilerParams(vmem_limit_bytes=VMEM_BYTES),
    )(*args)


def pack_kernel(scal, spec, to_prev, to_next):
    cols = lax.broadcasted_iota(jnp.int32, (ROWS, M), 1)
    for part in range(2):
        left = spec[part, :, :M]
        right = spec[part, :, M:]
        to_prev[part] = jnp.where(cols >= scal[4], left, right)
        to_next[part] = jnp.where(cols >= scal[6], left, right)


def pupil_kernel(scal, pupil, amplitude, rolled, other_amp):
    parity = scal[0]
    shift = lax.rem(scal[2], M)
    down = lax.rem(scal[1] - parity * ROWS + M, M)
    for part in range(2):
        rolled[part] = pltpu.roll(pltpu.roll(pupil[part], shift, 1), down, 0)[:ROWS]
    other_amp[...] = jnp.where(parity == 0, amplitude[:, ROWS:], amplitude[:, :ROWS])


def first_kernel(scal, spec, below, above, pupil, table, keep, send):
    parity = scal[0]
    base = parity * ROWS
    cols = lax.broadcasted_iota(jnp.int32, (ROWS, M), 1)
    rows = lax.broadcasted_iota(jnp.int32, (ROWS, M), 0) + base
    field = []
    for part in range(2):
        own = jnp.where(cols >= scal[2], spec[part, :, :M], spec[part, :, M:])
        field.append(
            jnp.where(rows < scal[1], below[part], jnp.where(rows >= scal[1] + M, above[part], own))
        )
    re = split(pupil[0] * field[0] - pupil[1] * field[1])
    im = split(pupil[0] * field[1] + pupil[1] * field[0])
    for out, half in ((send, 1 - parity), (keep, parity)):
        where = pl.ds(pl.multiple_of(half * ROWS, ROWS), ROWS)
        cos = (table[0, where, :], table[1, where, :])
        sin = (table[2, where, :], table[3, where, :])
        res = complex_times_rows(re, im, cos, sin)
        out[0], out[1] = res


def mmt(left, right):
    return lax.dot_general(left, right, (((1,), (1,)), ((), ())), preferred_element_type=F32)


def mmt3(left, right):
    return mmt(left[0], right[0]) + mmt(left[0], right[1]) + mmt(left[1], right[0])


def complex_times_rows(re, im, cos, sin):
    return mmt3(re, cos) - mmt3(im, sin), mmt3(re, sin) + mmt3(im, cos)


def second_kernel(scal, keep, other, amplitude, other_amp, table, keep_out, send_out):
    parity = scal[0]
    mine = pl.ds(pl.multiple_of(parity * ROWS, ROWS), ROWS)
    yours = pl.ds(pl.multiple_of((1 - parity) * ROWS, ROWS), ROWS)
    low = parity == 0
    pair = []
    for part in range(2):
        top = jnp.where(low, keep[part], other[part])
        bottom = jnp.where(low, other[part], keep[part])
        pair.append(split(jnp.concatenate([top, bottom], axis=0)))
    cos = (table[0], table[1])
    sin = (table[2], table[3])
    wave_re, wave_im = table_times_complex(cos, sin, 1, *pair)
    measured = jnp.where(low, amplitude[:, :ROWS], amplitude[:, ROWS:]) + other_amp[...]
    modulus = jnp.sqrt(wave_re * wave_re + wave_im * wave_im + GAMMA)
    keeping = 1.0 - measured / modulus
    fit_re = split(wave_re * keeping)
    fit_im = split(wave_im * keeping)
    for out, where in ((send_out, yours), (keep_out, mine)):
        cos = (table[0, where, :], table[1, where, :])
        sin = (table[2, where, :], table[3, where, :])
        res = table_times_complex(cos, sin, -1, fit_re, fit_im)
        out[0], out[1] = res


def third_kernel(scal, keep, other, pupil, table, grad):
    low = scal[0] == 0
    pair = []
    for part in range(2):
        left = jnp.where(low, keep[part], other[part])
        right = jnp.where(low, other[part], keep[part])
        pair.append(split(jnp.concatenate([left, right], axis=1)))
    cos = (table[0], table[1])
    sin = (table[2], table[3])
    back_re, back_im = complex_times_table(*pair, cos, sin, -1)
    grad[0] = pupil[0] * back_re + pupil[1] * back_im
    grad[1] = pupil[0] * back_im - pupil[1] * back_re


def gather_kernel(scal, own, from_prev, from_next, total, outgoing):
    base = scal[0] * ROWS
    cols = lax.broadcasted_iota(jnp.int32, (LOW, M), 1)
    for at in range(N_COL):
        rows = lax.broadcasted_iota(jnp.int32, (LOW, M), 0) + base + at * LOW
        here = pl.ds(at * LOW, LOW)
        own_rows = jnp.logical_and(rows >= scal[1], rows < scal[1] + M)
        prev_rows = rows < scal[3]
        next_rows = rows >= scal[5] + M
        for part in range(2):
            mine = jnp.where(own_rows, own[part, here, :], 0.0)
            prev = jnp.where(prev_rows, from_prev[part, here, :], 0.0)
            nxt = jnp.where(next_rows, from_next[part, here, :], 0.0)
            left = (
                jnp.where(cols >= scal[2], mine, 0.0)
                + jnp.where(cols >= scal[4], prev, 0.0)
                + jnp.where(cols >= scal[6], nxt, 0.0)
            )
            right = (
                jnp.where(cols < scal[2], mine, 0.0)
                + jnp.where(cols < scal[4], prev, 0.0)
                + jnp.where(cols < scal[6], nxt, 0.0)
            )
            total[part, here, :M] = left
            total[part, here, M:] = right
            outgoing[at, part, :, :M] = left
            outgoing[at, part, :, M:] = right


def rows_kernel(pencil, twist, table, outgoing, digits):
    for group in range(LOW // 8):
        for tile in range(2):
            lanes = slice(tile * 128, tile * 128 + 128)
            values = [
                tuple(
                    pencil[
                        at // 4,
                        part,
                        group * 8 : group * 8 + 8,
                        (at % 4) * 256 + tile * 128 : (at % 4) * 256 + tile * 128 + 128,
                    ]
                    for part in range(2)
                )
                for at in range(LOW)
            ]
            for at, (re, im) in enumerate(fft_list(values)):
                cos = twist[0, at : at + 1, lanes]
                sin = twist[1, at : at + 1, lanes]
                place = pl.ds((at // 8) * 256 + group * 64 + at % 8, 8, 8)
                digits[tile, place, :] = re * cos - im * sin
                digits[2 + tile, place, :] = re * sin + im * cos
    re = split(jnp.concatenate([digits[0], digits[1]], axis=1))
    im = split(jnp.concatenate([digits[2], digits[3]], axis=1))
    cos = (table[0], table[1])
    sin = (table[2], table[3])
    for part, flat in enumerate(complex_times_table(re, im, cos, sin, 1)):
        turned = flat.T
        for at in range(8):
            outgoing[pl.ds(part * 8 + at, PARTS, 16), :] = turned[:, at * 128 : at * 128 + 128]


def final_kernel(incoming, twist, table, image, digits):
    pair = []
    for part in range(2):
        flat = jnp.concatenate([incoming[pl.ds(part * 8 + at, PARTS, 16), :] for at in range(8)], axis=1)
        pair.append(split(flat.T))
    cos = (table[0], table[1])
    sin = (table[2], table[3])
    digits[0], digits[1] = complex_times_table(*pair, cos, sin, 1)
    for group in range(LOW // 8):
        for tile in range(2):
            lanes = slice(tile * 128, tile * 128 + 128)
            values = []
            for at in range(LOW):
                rows = slice(group * 256 + at * 8, group * 256 + at * 8 + 8)
                re = digits[0, rows, lanes]
                im = digits[1, rows, lanes]
                cos = twist[0, at : at + 1, lanes]
                sin = twist[1, at : at + 1, lanes]
                values.append((re * cos - im * sin, re * sin + im * cos))
            for at, value in enumerate(fft_list(values)):
                for part in range(2):
                    image[
                        part,
                        group * 8 : group * 8 + 8,
                        at * 256 + tile * 128 : at * 256 + tile * 128 + 128,
                    ] = value[part]


def stepped(by, odd_only=False):
    return [(i, i + by) for i in range(N_ROW) if 0 <= i + by < N_ROW and not (odd_only and i % 2 == 0)]


PARTNERS = [(i, i ^ 1) for i in range(N_ROW)]


def on_device(spectrum, pupil, amplitude, offsets, holds, window_table, part_table, twist):
    row = lax.axis_index("row")
    col = lax.axis_index("col")
    corner = offsets[0, 0]
    prev_corner = lax.ppermute(corner, "row", stepped(2))
    next_corner = lax.ppermute(corner, "row", stepped(-2))
    pair_row = (row // 2) * M
    scal = jnp.stack(
        [
            row % 2,
            corner[0] - pair_row,
            corner[1] - col * COLS,
            prev_corner[0] - pair_row + M,
            prev_corner[1] - col * COLS,
            next_corner[0] - pair_row - M,
            next_corner[1] - col * COLS,
            holds[0, 0],
        ]
    )
    measured = amplitude[0, 0]
    half = (2, ROWS, M)
    quarter = (2, ROWS, ROWS)

    to_prev, to_next = call(pack_kernel, [half, half], (0,), scal, spectrum)()
    below = lax.ppermute(to_prev, "row", stepped(-2))
    above = lax.ppermute(to_next, "row", stepped(2, odd_only=True))
    rolled, amp_out = call(pupil_kernel, [half, (M, ROWS)], (0,), scal, pupil, measured)()
    other_amp = lax.ppermute(amp_out, "row", PARTNERS)

    keep, send = call(first_kernel, [quarter, quarter], (0,), scal, spectrum, below, above, rolled, window_table)()
    other = lax.ppermute(send, "row", PARTNERS)
    keep, send = call(
        second_kernel, [quarter, quarter], (0,), scal, keep, other, measured, other_amp, window_table
    )()
    other = lax.ppermute(send, "row", PARTNERS)
    (grad,) = call(third_kernel, [half], (0,), scal, keep, other, rolled, window_table)()

    from_prev = lax.ppermute(grad, "row", stepped(2))
    from_next = lax.ppermute(grad, "row", stepped(-2, odd_only=True))
    total, outgoing = call(
        gather_kernel,
        [(2, ROWS, COLS), (N_COL, 2, LOW, COLS)],
        (0,),
        scal,
        grad,
        from_prev,
        from_next,
    )()
    pencil = lax.all_to_all(outgoing, "col", split_axis=0, concat_axis=0, tiled=True)
    (outgoing,) = call(rows_kernel, [(PARTS * 16, 128)], (), pencil, twist, part_table)(
        [pltpu.VMEM((4, COLS, 128), F32)]
    )
    incoming = lax.all_to_all(
        outgoing.reshape(PARTS, 16, 128), ("row", "col"), split_axis=0, concat_axis=0, tiled=True
    ).reshape(PARTS * 16, 128)
    (image,) = call(final_kernel, [(2, LOW, N)], (), incoming, twist, part_table)(
        [pltpu.VMEM((2, COLS, PARTS), F32)]
    )
    return (total, image)


def solution(mesh):
    window_table = dft_tables(M, 1.0 / math.sqrt(M))
    part_table = dft_tables(PARTS, 1.0 / math.sqrt(N))
    twist = twist_tables()
    mapped = jax.shard_map(
        on_device,
        mesh=mesh,
        in_specs=(
            P(None, "row", "col"),
            P(),
            P("row", "col", None, None),
            P("row", "col", None),
            P("row", "col"),
            P(),
            P(),
            P(),
        ),
        out_specs=(P(None, "row", "col"), P(None, ("row", "col"), None)),
        check_vma=False,
    )

    def run(spectrum, pupil, amplitude, offsets, holds):
        return mapped(
            spectrum,
            pupil,
            amplitude,
            offsets,
            holds,
            jnp.asarray(window_table),
            jnp.asarray(part_table),
            jnp.asarray(twist),
        )

    return run
```

```python
import math

import jax
import jax.numpy as jnp
import ml_dtypes
import numpy as np
from jax import lax
from jax.experimental import pallas as pl
from jax.experimental.pallas import tpu as pltpu
from jax.sharding import PartitionSpec as P

GAMMA = 1.0
N = 8192
M = 512
ROWS = 256
COLS = 1024
N_ROW = 32
N_COL = 8
PARTS = N_ROW * N_COL
LOW = 32
F32 = jnp.float32
BF16 = jnp.bfloat16
VMEM_BYTES = 32 * 1024 * 1024


def halves(table):
    high = table.astype(np.float32).astype(ml_dtypes.bfloat16)
    low = (table - high.astype(np.float64)).astype(np.float32).astype(ml_dtypes.bfloat16)
    return high, low


def dft_tables(length, scale):
    counter = np.arange(length)
    angles = 2.0 * np.pi / length * (np.outer(counter, counter) % length)
    return np.stack(halves(np.cos(angles) * scale) + halves(np.sin(angles) * scale))


def twist_tables():
    angles = 2.0 * np.pi / N * np.outer(np.arange(LOW), np.arange(PARTS))
    return np.stack([np.cos(angles), np.sin(angles)]).astype(np.float32)


def split(values):
    high = values.astype(BF16)
    low = (values - high.astype(F32)).astype(BF16)
    return high, low


def mm(left, right):
    return jnp.dot(left, right, preferred_element_type=F32)


def mm3(left, right):
    return mm(left[0], right[0]) + mm(left[0], right[1]) + mm(left[1], right[0])


def complex_times_table(re, im, cos, sin, sign):
    rc, rs, ic, is_ = mm3(re, cos), mm3(re, sin), mm3(im, cos), mm3(im, sin)
    if sign > 0:
        return rc - is_, rs + ic
    return rc + is_, ic - rs


def table_times_complex(cos, sin, sign, re, im):
    rc, rs, ic, is_ = mm3(cos, re), mm3(sin, re), mm3(cos, im), mm3(sin, im)
    if sign > 0:
        return rc - is_, rs + ic
    return rc + is_, ic - rs


def turn(value, numer, denom):
    re, im = value
    numer %= denom
    if numer == 0:
        return re, im
    if 4 * numer == denom:
        return -im, re
    if 2 * numer == denom:
        return -re, -im
    cos = math.cos(2.0 * math.pi * numer / denom)
    sin = math.sin(2.0 * math.pi * numer / denom)
    if 8 * numer == denom:
        return (re - im) * cos, (re + im) * cos
    if 8 * numer == 3 * denom:
        return (re + im) * -sin, (re - im) * sin
    return re * cos - im * sin, re * sin + im * cos


def fft_list(values):
    count = len(values)
    if count == 1:
        return values
    even = fft_list(values[0::2])
    odd = fft_list(values[1::2])
    first, second = [], []
    for at in range(count // 2):
        er, ei = even[at]
        tr, ti = turn(odd[at], at, count)
        first.append((er + tr, ei + ti))
        second.append((er - tr, ei - ti))
    return first + second


def call(kernel, outs, smem, *args):
    specs = [pl.BlockSpec(memory_space=pltpu.SMEM if at in smem else pltpu.VMEM) for at in range(len(args))]
    return lambda scratch=(): pl.pallas_call(
        kernel,
        out_shape=tuple(jax.ShapeDtypeStruct(shape, F32) for shape in outs),
        in_specs=specs,
        out_specs=tuple(pl.BlockSpec(memory_space=pltpu.VMEM) for _ in outs),
        scratch_shapes=scratch,
        compiler_params=pltpu.CompilerParams(vmem_limit_bytes=VMEM_BYTES),
    )(*args)


def frame(pos, corner):
    return corner[0] - pos[0] * ROWS, corner[1] - pos[1] * COLS


def corners(pos, local, lower, upper):
    moved = jnp.logical_and(lax.rem(pos[0], 2) == 0, lax.rem(pos[1], 2) == 1)
    local, lower, upper = frame(pos, local), frame(pos, lower), frame(pos, upper)
    here = tuple(jnp.where(moved, x, y) for x, y in zip(lower, local))
    up = tuple(jnp.where(moved, x, y) for x, y in zip(local, upper))
    return here, lower, up


def inside(rows, start):
    return jnp.logical_and(rows >= start, rows < start + M)


def pack_kernel(pos, local, lower, upper, spec, to_lower, to_upper):
    _, down, up = corners(pos, local, lower, upper)
    cols = lax.broadcasted_iota(jnp.int32, (ROWS, M), 1)
    for part in range(2):
        left = spec[part, :, :M]
        right = spec[part, :, M:]
        to_lower[part] = jnp.where(cols >= down[1], left, right)
        to_upper[part] = jnp.where(cols >= up[1], left, right)


def pupil_kernel(pos, local, lower, upper, pupil, rolled):
    (at_row, at_col), _, _ = corners(pos, local, lower, upper)
    shift = lax.rem(at_col, M)
    down = lax.rem(at_row + 2 * N, M)
    for part in range(2):
        rolled[part] = pltpu.roll(pltpu.roll(pupil[part], shift, 1), down, 0)[:ROWS]


def first_kernel(pos, local, lower, upper, spec, from_lower, from_upper, pupil, table, keep, send):
    parity = lax.rem(pos[0], 2)
    (at_row, at_col), _, _ = corners(pos, local, lower, upper)
    cols = lax.broadcasted_iota(jnp.int32, (ROWS, M), 1)
    rows = lax.broadcasted_iota(jnp.int32, (ROWS, M), 0)
    field = []
    for part in range(2):
        own = jnp.where(cols >= at_col, spec[part, :, :M], spec[part, :, M:])
        other = jnp.where(inside(rows + M, at_row), from_upper[part], from_lower[part])
        field.append(jnp.where(inside(rows, at_row), own, other))
    re = split(pupil[0] * field[0] - pupil[1] * field[1])
    im = split(pupil[0] * field[1] + pupil[1] * field[0])
    for out, half in ((send, 1 - parity), (keep, parity)):
        where = pl.ds(pl.multiple_of(half * ROWS, ROWS), ROWS)
        cos = (table[0, where, :], table[1, where, :])
        sin = (table[2, where, :], table[3, where, :])
        out[0], out[1] = complex_times_rows(re, im, cos, sin)


def mmt(left, right):
    return lax.dot_general(left, right, (((1,), (1,)), ((), ())), preferred_element_type=F32)


def mmt3(left, right):
    return mmt(left[0], right[0]) + mmt(left[0], right[1]) + mmt(left[1], right[0])


def complex_times_rows(re, im, cos, sin):
    return mmt3(re, cos) - mmt3(im, sin), mmt3(re, sin) + mmt3(im, cos)


def second_kernel(pos, keep, other, amplitude, near_amp, far_amp, table, keep_out, send_out):
    parity = lax.rem(pos[0], 2)
    moved = jnp.logical_and(parity == 0, lax.rem(pos[1], 2) == 1)
    mine = pl.ds(pl.multiple_of(parity * ROWS, ROWS), ROWS)
    yours = pl.ds(pl.multiple_of((1 - parity) * ROWS, ROWS), ROWS)
    low = parity == 0
    pair = []
    for part in range(2):
        top = jnp.where(low, keep[part], other[part])
        bottom = jnp.where(low, other[part], keep[part])
        pair.append(split(jnp.concatenate([top, bottom], axis=0)))
    cos = (table[0], table[1])
    sin = (table[2], table[3])
    wave_re, wave_im = table_times_complex(cos, sin, 1, *pair)
    measured = jnp.where(low, amplitude[:, :ROWS], amplitude[:, ROWS:])
    measured = jnp.where(moved, far_amp[...], measured) + near_amp[...]
    modulus = jnp.sqrt(wave_re * wave_re + wave_im * wave_im + GAMMA)
    keeping = 1.0 - measured / modulus
    fit_re = split(wave_re * keeping)
    fit_im = split(wave_im * keeping)
    for out, where in ((send_out, yours), (keep_out, mine)):
        cos = (table[0, where, :], table[1, where, :])
        sin = (table[2, where, :], table[3, where, :])
        out[0], out[1] = table_times_complex(cos, sin, -1, fit_re, fit_im)


def third_kernel(pos, keep, other, pupil, table, grad_re, grad_im):
    low = lax.rem(pos[0], 2) == 0
    pair = []
    for part in range(2):
        left = jnp.where(low, keep[part], other[part])
        right = jnp.where(low, other[part], keep[part])
        pair.append(split(jnp.concatenate([left, right], axis=1)))
    cos = (table[0], table[1])
    sin = (table[2], table[3])
    back_re, back_im = complex_times_table(*pair, cos, sin, -1)
    grad_re[...] = pupil[0] * back_re + pupil[1] * back_im
    grad_im[...] = pupil[0] * back_im - pupil[1] * back_re


def gather_kernel(pos, local, lower, upper, own, from_lower, from_upper, total):
    leds = corners(pos, local, lower, upper)
    cols = lax.broadcasted_iota(jnp.int32, (LOW, M), 1)
    for at in range(N_COL):
        rows = lax.broadcasted_iota(jnp.int32, (LOW, M), 0) + at * LOW
        here = pl.ds(at * LOW, LOW)
        left = right = 0.0
        for (at_row, at_col), source in zip(leds, (own, from_lower, from_upper)):
            value = jnp.where(inside(rows, at_row), source[here, :], 0.0)
            left = left + jnp.where(cols >= at_col, value, 0.0)
            right = right + jnp.where(cols < at_col, value, 0.0)
        total[here, :M] = left
        total[here, M:] = right


def rows_kernel(pencil_re, pencil_im, twist, table, outgoing, digits):
    for group in range(LOW // 8):
        for tile in range(2):
            lanes = slice(tile * 128, tile * 128 + 128)
            values = [
                tuple(
                    pencil[
                        at // 4,
                        group * 8 : group * 8 + 8,
                        (at % 4) * 256 + tile * 128 : (at % 4) * 256 + tile * 128 + 128,
                    ]
                    for pencil in (pencil_re, pencil_im)
                )
                for at in range(LOW)
            ]
            for at, (re, im) in enumerate(fft_list(values)):
                cos = twist[0, at : at + 1, lanes]
                sin = twist[1, at : at + 1, lanes]
                place = pl.ds((at // 8) * 256 + group * 64 + at % 8, 8, 8)
                digits[tile, place, :] = re * cos - im * sin
                digits[2 + tile, place, :] = re * sin + im * cos
    re = split(jnp.concatenate([digits[0], digits[1]], axis=1))
    im = split(jnp.concatenate([digits[2], digits[3]], axis=1))
    cos = (table[0], table[1])
    sin = (table[2], table[3])
    for part, flat in enumerate(complex_times_table(re, im, cos, sin, 1)):
        turned = flat.T
        for at in range(8):
            outgoing[pl.ds(part * 8 + at, PARTS, 16), :] = turned[:, at * 128 : at * 128 + 128]


def final_kernel(incoming, twist, table, image, digits):
    pair = []
    for part in range(2):
        flat = jnp.concatenate([incoming[pl.ds(part * 8 + at, PARTS, 16), :] for at in range(8)], axis=1)
        pair.append(split(flat.T))
    cos = (table[0], table[1])
    sin = (table[2], table[3])
    digits[0], digits[1] = complex_times_table(*pair, cos, sin, 1)
    for group in range(LOW // 8):
        for tile in range(2):
            lanes = slice(tile * 128, tile * 128 + 128)
            values = []
            for at in range(LOW):
                rows = slice(group * 256 + at * 8, group * 256 + at * 8 + 8)
                re = digits[0, rows, lanes]
                im = digits[1, rows, lanes]
                cos = twist[0, at : at + 1, lanes]
                sin = twist[1, at : at + 1, lanes]
                values.append((re * cos - im * sin, re * sin + im * cos))
            for at, value in enumerate(fft_list(values)):
                for part in range(2):
                    image[
                        part,
                        group * 8 : group * 8 + 8,
                        at * 256 + tile * 128 : at * 256 + tile * 128 + 128,
                    ] = value[part]


def moves(rule):
    pairs = [(row, col, rule(row, col % 2)) for row in range(N_ROW) for col in range(N_COL)]
    return [(row * N_COL + col, to * N_COL + col) for row, col, to in pairs if to is not None]


def downward(row, core):
    return row - 2 if row >= 2 and (row % 2 == 1 or core == 0) else None


def upward(row, core):
    if row % 2 == 0:
        return (row + 2) % N_ROW if core == 1 else None
    return row + 2 if row + 2 < N_ROW else None


def partner(row, core):
    return row ^ 1 if core == 0 else (row + (1 if row % 2 == 1 else -1)) % N_ROW


def near(row, core):
    return row ^ 1 if core == 0 else (row + 1) % N_ROW


def far(row, core):
    return (row + 2) % N_ROW if core == 1 and row % 2 == 0 else None


def back(pairs):
    return [(to, source) for source, to in pairs]


BOTH = ("row", "col")
DOWN = moves(downward)
UP = moves(upward)
PARTNERS = moves(partner)
NEAR = moves(near)
FAR = moves(far)
FROM_LOWER = moves(lambda row, core: (row + 2) % N_ROW)
FROM_UPPER = moves(lambda row, core: row - 2 if row >= 2 and row % 2 == 1 else None)


def on_device(spectrum, pupil, amplitude, offsets, holds, window_table, part_table, twist):
    row = lax.axis_index("row")
    col = lax.axis_index("col")
    pos = jnp.stack([row, col]).astype(jnp.int32)
    local = offsets[0, 0]
    lower = lax.ppermute(local, BOTH, FROM_LOWER)
    upper = lax.ppermute(local, BOTH, FROM_UPPER)
    where = (pos, local, lower, upper)
    smem = (0, 1, 2, 3)
    measured = amplitude[0, 0]
    half = (ROWS, M)
    quarter = (2, ROWS, ROWS)
    near_half = lax.dynamic_slice(measured, (jnp.int32(0), (1 - row % 2) * ROWS), (M, ROWS))
    near_amp = lax.ppermute(near_half, BOTH, NEAR)
    far_amp = lax.ppermute(measured[:, :ROWS], BOTH, FAR)

    to_lower, to_upper = call(pack_kernel, [(2,) + half, (2,) + half], smem, *where, spectrum)()
    from_upper = lax.ppermute(to_lower, BOTH, DOWN)
    from_lower = lax.ppermute(to_upper, BOTH, UP)
    (rolled,) = call(pupil_kernel, [(2,) + half], smem, *where, pupil)()

    keep, send = call(
        first_kernel, [quarter, quarter], smem, *where, spectrum, from_lower, from_upper, rolled, window_table
    )()
    other = lax.ppermute(send, BOTH, PARTNERS)
    keep, send = call(
        second_kernel, [quarter, quarter], (0,), pos, keep, other, measured, near_amp, far_amp, window_table
    )()
    other = lax.ppermute(send, BOTH, PARTNERS)
    grads = call(third_kernel, [half, half], (0,), pos, keep, other, rolled, window_table)()

    moved = [(lax.ppermute(grad, BOTH, back(DOWN)), lax.ppermute(grad, BOTH, back(UP))) for grad in grads]
    totals, pencils = [], []
    for grad, sources in zip(grads, moved):
        (total,) = call(gather_kernel, [(ROWS, COLS)], smem, *where, grad, *sources)()
        totals.append(total)
        pencils.append(
            lax.all_to_all(total.reshape(N_COL, LOW, COLS), "col", split_axis=0, concat_axis=0, tiled=True)
        )
    (outgoing,) = call(rows_kernel, [(PARTS * 16, 128)], (), *pencils, twist, part_table)(
        [pltpu.VMEM((4, COLS, 128), F32)]
    )
    incoming = lax.all_to_all(
        outgoing.reshape(PARTS, 16, 128), ("row", "col"), split_axis=0, concat_axis=0, tiled=True
    ).reshape(PARTS * 16, 128)
    (image,) = call(final_kernel, [(2, LOW, N)], (), incoming, twist, part_table)(
        [pltpu.VMEM((2, COLS, PARTS), F32)]
    )
    return (jnp.stack(totals), image)


def solution(mesh):
    window_table = dft_tables(M, 1.0 / math.sqrt(M))
    part_table = dft_tables(PARTS, 1.0 / math.sqrt(N))
    twist = twist_tables()
    mapped = jax.shard_map(
        on_device,
        mesh=mesh,
        in_specs=(
            P(None, "row", "col"),
            P(),
            P("row", "col", None, None),
            P("row", "col", None),
            P("row", "col"),
            P(),
            P(),
            P(),
        ),
        out_specs=(P(None, "row", "col"), P(None, ("row", "col"), None)),
        check_vma=False,
    )

    def run(spectrum, pupil, amplitude, offsets, holds):
        return mapped(
            spectrum,
            pupil,
            amplitude,
            offsets,
            holds,
            jnp.asarray(window_table),
            jnp.asarray(part_table),
            jnp.asarray(twist),
        )

    return run
```

```python
import math

import jax
import jax.numpy as jnp
import ml_dtypes
import numpy as np
from jax import lax
from jax.experimental import pallas as pl
from jax.experimental.pallas import tpu as pltpu
from jax.sharding import PartitionSpec as P

GAMMA = 1.0
N = 8192
M = 512
ROWS = 256
COLS = 1024
N_ROW = 32
N_COL = 8
PARTS = N_ROW * N_COL
LOW = 32
ORDER = [0, 2, 4, 6, 1, 3, 5, 7]
F32 = jnp.float32
BF16 = jnp.bfloat16
SLOW = 10**11
VMEM_BYTES = 32 * 1024 * 1024


def halves(table):
    high = table.astype(np.float32).astype(ml_dtypes.bfloat16)
    low = (table - high.astype(np.float64)).astype(np.float32).astype(ml_dtypes.bfloat16)
    return high, low


def dft_tables(length, scale):
    counter = np.arange(length)
    angles = 2.0 * np.pi / length * (np.outer(counter, counter) % length)
    return np.stack(halves(np.cos(angles) * scale) + halves(np.sin(angles) * scale))


def twist_tables():
    angles = 2.0 * np.pi / N * np.outer(np.arange(LOW), np.arange(PARTS))
    return np.stack([np.cos(angles), np.sin(angles)]).astype(np.float32)


def split(values):
    high = values.astype(BF16)
    low = (values - high.astype(F32)).astype(BF16)
    return high, low


def mm(left, right):
    return jnp.dot(left, right, preferred_element_type=F32)


def mm3(left, right):
    return mm(left[0], right[0]) + mm(left[0], right[1]) + mm(left[1], right[0])


def complex_times_table(re, im, cos, sin, sign):
    rc, rs, ic, is_ = mm3(re, cos), mm3(re, sin), mm3(im, cos), mm3(im, sin)
    if sign > 0:
        return rc - is_, rs + ic
    return rc + is_, ic - rs


def table_times_complex(cos, sin, sign, re, im):
    rc, rs, ic, is_ = mm3(cos, re), mm3(sin, re), mm3(cos, im), mm3(sin, im)
    if sign > 0:
        return rc - is_, rs + ic
    return rc + is_, ic - rs


def turn(value, numer, denom):
    re, im = value
    numer %= denom
    if numer == 0:
        return re, im
    if 4 * numer == denom:
        return -im, re
    if 2 * numer == denom:
        return -re, -im
    cos = math.cos(2.0 * math.pi * numer / denom)
    sin = math.sin(2.0 * math.pi * numer / denom)
    if 8 * numer == denom:
        return (re - im) * cos, (re + im) * cos
    if 8 * numer == 3 * denom:
        return (re + im) * -sin, (re - im) * sin
    return re * cos - im * sin, re * sin + im * cos


def fft_list(values):
    count = len(values)
    if count == 1:
        return values
    even = fft_list(values[0::2])
    odd = fft_list(values[1::2])
    first, second = [], []
    for at in range(count // 2):
        er, ei = even[at]
        tr, ti = turn(odd[at], at, count)
        first.append((er + tr, ei + ti))
        second.append((er - tr, ei - ti))
    return first + second


def call(kernel, outs, smem, *args, cost=None):
    specs = [pl.BlockSpec(memory_space=pltpu.SMEM if at in smem else pltpu.VMEM) for at in range(len(args))]
    return lambda scratch=(): pl.pallas_call(
        kernel,
        out_shape=tuple(jax.ShapeDtypeStruct(shape, F32) for shape in outs),
        in_specs=specs,
        out_specs=tuple(pl.BlockSpec(memory_space=pltpu.VMEM) for _ in outs),
        scratch_shapes=scratch,
        cost_estimate=cost and pl.CostEstimate(flops=cost, bytes_accessed=0, transcendentals=0),
        compiler_params=pltpu.CompilerParams(vmem_limit_bytes=VMEM_BYTES),
    )(*args)


def frame(pos, corner):
    return corner[0] - pos[0] * ROWS, corner[1] - pos[1] * COLS


def corners(pos, local, lower, upper):
    moved = jnp.logical_and(lax.rem(pos[0], 2) == 0, lax.rem(pos[1], 2) == 1)
    local, lower, upper = frame(pos, local), frame(pos, lower), frame(pos, upper)
    here = tuple(jnp.where(moved, x, y) for x, y in zip(lower, local))
    up = tuple(jnp.where(moved, x, y) for x, y in zip(local, upper))
    return here, lower, up


def inside(rows, start):
    return jnp.logical_and(rows >= start, rows < start + M)


def pack_kernel(pos, local, lower, upper, spec, to_lower, to_upper):
    _, down, up = corners(pos, local, lower, upper)
    cols = lax.broadcasted_iota(jnp.int32, (ROWS, M), 1)
    for part in range(2):
        left = spec[part, :, :M]
        right = spec[part, :, M:]
        to_lower[part] = jnp.where(cols >= down[1], left, right)
        to_upper[part] = jnp.where(cols >= up[1], left, right)


def pupil_kernel(pos, local, lower, upper, pupil, rolled):
    (at_row, at_col), _, _ = corners(pos, local, lower, upper)
    shift = lax.rem(at_col, M)
    down = lax.rem(at_row + 2 * N, M)
    for part in range(2):
        rolled[part] = pltpu.roll(pltpu.roll(pupil[part], shift, 1), down, 0)[:ROWS]


def stage_kernel(spec, staged):
    staged[...] = spec[...]


def half_rows(table, half):
    where = pl.ds(pl.multiple_of(half * ROWS, ROWS), ROWS)
    return (table[0, where, :], table[1, where, :]), (table[2, where, :], table[3, where, :])


def half_cols(table, half):
    where = pl.ds(pl.multiple_of(half * ROWS, ROWS), ROWS)
    return (table[0, :, where], table[1, :, where]), (table[2, :, where], table[3, :, where])


def field_of(where, spec, from_lower, from_upper, pupil):
    (at_row, at_col), _, _ = corners(*where)
    cols = lax.broadcasted_iota(jnp.int32, (ROWS, M), 1)
    rows = lax.broadcasted_iota(jnp.int32, (ROWS, M), 0)
    field = []
    for part in range(2):
        own = jnp.where(cols >= at_col, spec[part, :, :M], spec[part, :, M:])
        other = jnp.where(inside(rows + M, at_row), from_upper[part], from_lower[part])
        field.append(jnp.where(inside(rows, at_row), own, other))
    re = split(pupil[0] * field[0] - pupil[1] * field[1])
    im = split(pupil[0] * field[1] + pupil[1] * field[0])
    return re, im


def send_kernel(pos, local, lower, upper, spec, from_lower, from_upper, pupil, table, send):
    re, im = field_of((pos, local, lower, upper), spec, from_lower, from_upper, pupil)
    cos, sin = half_cols(table, 1 - lax.rem(pos[0], 2))
    send[0], send[1] = complex_times_table(re, im, cos, sin, 1)


def keep_kernel(pos, local, lower, upper, spec, from_lower, from_upper, pupil, table, wave):
    parity = lax.rem(pos[0], 2)
    re, im = field_of((pos, local, lower, upper), spec, from_lower, from_upper, pupil)
    cos, sin = half_cols(table, parity)
    re, im = complex_times_table(re, im, cos, sin, 1)
    wave[0], wave[1] = table_times_complex(cos, sin, 1, split(re), split(im))


def fit_kernel(pos, wave, other, amplitude, near_amp, far_amp, table, fit, send):
    parity = lax.rem(pos[0], 2)
    moved = jnp.logical_and(parity == 0, lax.rem(pos[1], 2) == 1)
    cos, sin = half_cols(table, 1 - parity)
    wave_re, wave_im = table_times_complex(cos, sin, 1, split(other[0]), split(other[1]))
    wave_re += wave[0]
    wave_im += wave[1]
    measured = jnp.where(parity == 0, amplitude[:, :ROWS], amplitude[:, ROWS:])
    measured = jnp.where(moved, far_amp[...], measured) + near_amp[...]
    modulus = jnp.sqrt(wave_re * wave_re + wave_im * wave_im + GAMMA)
    keeping = 1.0 - measured / modulus
    fit[0] = wave_re * keeping
    fit[1] = wave_im * keeping
    cos, sin = half_rows(table, 1 - parity)
    send[0], send[1] = table_times_complex(cos, sin, -1, split(fit[0]), split(fit[1]))


def stay_kernel(pos, fit, table, part):
    cos, sin = half_rows(table, lax.rem(pos[0], 2))
    re, im = table_times_complex(cos, sin, -1, split(fit[0]), split(fit[1]))
    part[0], part[1] = complex_times_table(split(re), split(im), cos, sin, -1)


def grad_kernel(pos, part, other, pupil, table, grad):
    cos, sin = half_rows(table, 1 - lax.rem(pos[0], 2))
    re, im = complex_times_table(split(other[0]), split(other[1]), cos, sin, -1)
    re += part[0]
    im += part[1]
    back_re = pupil[0] * re + pupil[1] * im
    back_im = pupil[0] * im - pupil[1] * re
    for at, col in enumerate(ORDER):
        grad[at, 0] = back_re[col * LOW : col * LOW + LOW]
        grad[at, 1] = back_im[col * LOW : col * LOW + LOW]


def rows_kernel(pos, leds, own, lower_even, lower_odd, upper_even, upper_odd, twist, table, outgoing, shares, pencil, digits):
    row, col = pos[0], pos[1]
    cols = lax.broadcasted_iota(jnp.int32, (LOW, M), 1)
    rows = lax.broadcasted_iota(jnp.int32, (LOW, M), 0) + col * LOW
    for at, source_col in enumerate(ORDER):
        lower, upper = (lower_even, upper_even) if at < 4 else (lower_odd, upper_odd)
        corner = [leds[source_col, index] for index in range(6)]
        around = corners((row, source_col), corner[:2], corner[2:4], corner[4:])
        place = lax.rem(source_col - col + N_COL, N_COL)
        for part in range(2):
            left = right = 0.0
            for (at_row, at_col), source in zip(around, (own[at, part], lower[at % 4, part], upper[at % 4, part])):
                value = jnp.where(inside(rows, at_row), source, 0.0)
                left = left + jnp.where(cols >= at_col, value, 0.0)
                right = right + jnp.where(cols < at_col, value, 0.0)
            pencil[source_col, part, :, :M] = left
            pencil[source_col, part, :, M:] = right
            shares[place, part, :, :M] = left
            shares[place, part, :, M:] = right
    for group in range(LOW // 8):
        for tile in range(2):
            lanes = slice(tile * 128, tile * 128 + 128)
            values = [
                tuple(
                    pencil[
                        at // 4,
                        part,
                        group * 8 : group * 8 + 8,
                        (at % 4) * 256 + tile * 128 : (at % 4) * 256 + tile * 128 + 128,
                    ]
                    for part in range(2)
                )
                for at in range(LOW)
            ]
            for at, (re, im) in enumerate(fft_list(values)):
                cos = twist[0, at : at + 1, lanes]
                sin = twist[1, at : at + 1, lanes]
                place = pl.ds((at // 8) * 256 + group * 64 + at % 8, 8, 8)
                digits[tile, place, :] = re * cos - im * sin
                digits[2 + tile, place, :] = re * sin + im * cos
    re = split(jnp.concatenate([digits[0], digits[1]], axis=1))
    im = split(jnp.concatenate([digits[2], digits[3]], axis=1))
    cos = (table[0], table[1])
    sin = (table[2], table[3])
    for part, flat in enumerate(complex_times_table(re, im, cos, sin, 1)):
        turned = flat.T
        for at in range(8):
            outgoing[pl.ds(part * 8 + at, PARTS, 16), :] = turned[:, at * 128 : at * 128 + 128]


def assemble_kernel(pos, *refs):
    total = refs[-1]
    for step, share in enumerate(refs[:-1]):
        where = pl.ds(pl.multiple_of(lax.rem(pos[1] - step + N_COL, N_COL) * LOW, LOW), LOW)
        for part in range(2):
            total[part, where, :] = share[part]


def final_kernel(incoming, twist, table, image, digits):
    pair = []
    for part in range(2):
        flat = jnp.concatenate([incoming[pl.ds(part * 8 + at, PARTS, 16), :] for at in range(8)], axis=1)
        pair.append(split(flat.T))
    cos = (table[0], table[1])
    sin = (table[2], table[3])
    digits[0], digits[1] = complex_times_table(*pair, cos, sin, 1)
    for group in range(LOW // 8):
        for tile in range(2):
            lanes = slice(tile * 128, tile * 128 + 128)
            values = []
            for at in range(LOW):
                rows = slice(group * 256 + at * 8, group * 256 + at * 8 + 8)
                re = digits[0, rows, lanes]
                im = digits[1, rows, lanes]
                cos = twist[0, at : at + 1, lanes]
                sin = twist[1, at : at + 1, lanes]
                values.append((re * cos - im * sin, re * sin + im * cos))
            for at, value in enumerate(fft_list(values)):
                for part in range(2):
                    image[
                        part,
                        group * 8 : group * 8 + 8,
                        at * 256 + tile * 128 : at * 256 + tile * 128 + 128,
                    ] = value[part]


def moves(rule):
    pairs = [(row, col, rule(row, col % 2)) for row in range(N_ROW) for col in range(N_COL)]
    return [(row * N_COL + col, to * N_COL + col) for row, col, to in pairs if to is not None]


def downward(row, core):
    return row - 2 if row >= 2 and (row % 2 == 1 or core == 0) else None


def upward(row, core):
    if row % 2 == 0:
        return (row + 2) % N_ROW if core == 1 else None
    return row + 2 if row + 2 < N_ROW else None


def partner(row, core):
    return row ^ 1 if core == 0 else (row + (1 if row % 2 == 1 else -1)) % N_ROW


def near(row, core):
    return row ^ 1 if core == 0 else (row + 1) % N_ROW


def far(row, core):
    return (row + 2) % N_ROW if core == 1 and row % 2 == 0 else None


BOTH = ("row", "col")
DOWN = moves(downward)
UP = moves(upward)
PARTNERS = moves(partner)
NEAR = moves(near)
FAR = moves(far)
FROM_LOWER = moves(lambda row, core: (row + 2) % N_ROW)
FROM_UPPER = moves(lambda row, core: row - 2 if row >= 2 and row % 2 == 1 else None)


def on_device(spectrum, pupil, amplitude, offsets, holds, window_table, part_table, twist):
    row = lax.axis_index("row")
    col = lax.axis_index("col")
    pos = jnp.stack([row, col]).astype(jnp.int32)
    local = offsets[0, 0]
    lower = lax.ppermute(local, BOTH, FROM_LOWER)
    upper = lax.ppermute(local, BOTH, FROM_UPPER)
    where = (pos, local, lower, upper)
    leds = lax.all_gather(jnp.concatenate([local, lower, upper]), "col")
    smem = (0, 1, 2, 3)
    measured = amplitude[0, 0]
    half = (ROWS, M)
    quarter = (2, ROWS, ROWS)
    near_half = lax.dynamic_slice(measured, (jnp.int32(0), (1 - row % 2) * ROWS), (M, ROWS))
    near_amp = lax.ppermute(near_half, BOTH, NEAR)
    far_amp = lax.ppermute(measured[:, :ROWS], BOTH, FAR)

    (staged,) = call(stage_kernel, [(2, ROWS, COLS)], (), spectrum)()
    to_lower, to_upper = call(pack_kernel, [(2,) + half, (2,) + half], smem, *where, staged)()
    from_upper = lax.ppermute(to_lower, BOTH, DOWN)
    from_lower = lax.ppermute(to_upper, BOTH, UP)
    (rolled,) = call(pupil_kernel, [(2,) + half], smem, *where, pupil)()

    sources = (*where, staged, from_lower, from_upper, rolled, window_table)
    (send,) = call(send_kernel, [quarter], smem, *sources)()
    other = lax.ppermute(send, BOTH, PARTNERS)
    (wave,) = call(keep_kernel, [(2, M, ROWS)], smem, *sources)()
    fit, send = call(
        fit_kernel, [(2, M, ROWS), quarter], (0,), pos, wave, other, measured, near_amp, far_amp, window_table
    )()
    other = lax.ppermute(send, BOTH, PARTNERS)
    (part,) = call(stay_kernel, [(2,) + half], (0,), pos, fit, window_table)()
    (grad,) = call(grad_kernel, [(N_COL, 2, LOW, M)], (0,), pos, part, other, rolled, window_table)()

    own = lax.all_to_all(grad, "col", split_axis=0, concat_axis=0, tiled=True, axis_index_groups=[ORDER])
    even, odd = own[:4], own[4:]
    lower_even = lax.ppermute(even, "row", [(row, row + 2) for row in range(N_ROW - 2)])
    upper_odd = lax.ppermute(odd, "row", [(row, row - 2) for row in range(2, N_ROW)] + [(0, N_ROW - 2)])
    lower_odd = lax.ppermute(odd, "row", [(row, row + 2) for row in range(1, N_ROW - 2, 2)])
    upper_even = lax.ppermute(even, "row", [(row, row - 2) for row in range(3, N_ROW, 2)])
    outgoing, shares = call(
        rows_kernel,
        [(PARTS * 16, 128), (N_COL, 2, LOW, COLS)],
        (0, 1),
        pos,
        leds,
        own,
        lower_even,
        lower_odd,
        upper_even,
        upper_odd,
        twist,
        part_table,
    )([pltpu.VMEM((N_COL, 2, LOW, COLS), F32), pltpu.VMEM((4, COLS, 128), F32)])
    back_shares = [shares[0]] + [
        lax.ppermute(shares[step], "col", [(at, (at + step) % N_COL) for at in range(N_COL)])
        for step in range(1, N_COL)
    ]
    (total,) = call(assemble_kernel, [(2, ROWS, COLS)], (0,), pos, *back_shares)()
    incoming = lax.all_to_all(
        outgoing.reshape(PARTS, 16, 128), ("row", "col"), split_axis=0, concat_axis=0, tiled=True
    ).reshape(PARTS * 16, 128)
    (image,) = call(final_kernel, [(2, LOW, N)], (), incoming, twist, part_table)(
        [pltpu.VMEM((2, COLS, PARTS), F32)]
    )
    return (total, image)


def solution(mesh):
    window_table = dft_tables(M, 1.0 / math.sqrt(M))
    part_table = dft_tables(PARTS, 1.0 / math.sqrt(N))
    twist = twist_tables()
    mapped = jax.shard_map(
        on_device,
        mesh=mesh,
        in_specs=(
            P(None, "row", "col"),
            P(),
            P("row", "col", None, None),
            P("row", "col", None),
            P("row", "col"),
            P(),
            P(),
            P(),
        ),
        out_specs=(P(None, "row", "col"), P(None, ("row", "col"), None)),
        check_vma=False,
    )

    def run(spectrum, pupil, amplitude, offsets, holds):
        return mapped(
            spectrum,
            pupil,
            amplitude,
            offsets,
            holds,
            jnp.asarray(window_table),
            jnp.asarray(part_table),
            jnp.asarray(twist),
        )

    return run
```

```python
import math

import jax
import jax.numpy as jnp
import ml_dtypes
import numpy as np
from jax import lax
from jax.experimental import pallas as pl
from jax.experimental.pallas import tpu as pltpu
from jax.sharding import PartitionSpec as P

GAMMA = 1.0
N = 8192
M = 512
ROWS = 256
COLS = 1024
N_ROW = 32
N_COL = 8
PARTS = N_ROW * N_COL
LOW = 32
ORDER = [0, 2, 4, 6, 1, 3, 5, 7]
F32 = jnp.float32
BF16 = jnp.bfloat16
VMEM_BYTES = 32 * 1024 * 1024
ROWS_VMEM_BYTES = 59 * 1024 * 1024


def halves(table):
    high = table.astype(np.float32).astype(ml_dtypes.bfloat16)
    low = (table - high.astype(np.float64)).astype(np.float32).astype(ml_dtypes.bfloat16)
    return high, low


def dft_tables(length, scale):
    counter = np.arange(length)
    angles = 2.0 * np.pi / length * (np.outer(counter, counter) % length)
    return np.stack(halves(np.cos(angles) * scale) + halves(np.sin(angles) * scale))


def twist_tables():
    angles = 2.0 * np.pi / N * np.outer(np.arange(LOW), np.arange(PARTS))
    return np.stack([np.cos(angles), np.sin(angles)]).astype(np.float32)


def split(values):
    high = values.astype(BF16)
    low = (values - high.astype(F32)).astype(BF16)
    return high, low


def mm(left, right):
    return jnp.dot(left, right, preferred_element_type=F32)


def six(first, second, axis):
    return jnp.concatenate([first[0], first[1], first[0], second[0], second[1], second[0]], axis=axis)


def six_table(first, second, axis):
    return jnp.concatenate([first[0], first[0], first[1], second[0], second[0], second[1]], axis=axis)


def minus(pair):
    return -pair[0], -pair[1]


def complex_times_table(re, im, cos, sin, sign):
    first, second = (minus(im), re) if sign > 0 else (im, minus(re))
    return (
        mm(six(re, first, 1), six_table(cos, sin, 0)),
        mm(six(second, im, 1), six_table(sin, cos, 0)),
    )


def table_times_complex(cos, sin, sign, re, im):
    first, second = (minus(im), re) if sign > 0 else (im, minus(re))
    return (
        mm(six_table(cos, sin, 1), six(re, first, 0)),
        mm(six_table(sin, cos, 1), six(second, im, 0)),
    )


def turn(value, numer, denom):
    re, im = value
    numer %= denom
    if numer == 0:
        return re, im
    if 4 * numer == denom:
        return -im, re
    if 2 * numer == denom:
        return -re, -im
    cos = math.cos(2.0 * math.pi * numer / denom)
    sin = math.sin(2.0 * math.pi * numer / denom)
    if 8 * numer == denom:
        return (re - im) * cos, (re + im) * cos
    if 8 * numer == 3 * denom:
        return (re + im) * -sin, (re - im) * sin
    return re * cos - im * sin, re * sin + im * cos


def fft_list(values):
    count = len(values)
    if count == 1:
        return values
    even = fft_list(values[0::2])
    odd = fft_list(values[1::2])
    first, second = [], []
    for at in range(count // 2):
        er, ei = even[at]
        tr, ti = turn(odd[at], at, count)
        first.append((er + tr, ei + ti))
        second.append((er - tr, ei - ti))
    return first + second


def call(kernel, outs, smem, *args, cost=None, hbm=False, limit=VMEM_BYTES):
    specs = [pl.BlockSpec(memory_space=pltpu.SMEM if at in smem else pltpu.VMEM) for at in range(len(args))]
    return lambda scratch=(): pl.pallas_call(
        kernel,
        out_shape=tuple(jax.ShapeDtypeStruct(shape, F32) for shape in outs),
        in_specs=specs,
        out_specs=tuple(pl.BlockSpec(memory_space=pltpu.HBM if hbm else pltpu.VMEM) for _ in outs),
        scratch_shapes=scratch,
        cost_estimate=cost and pl.CostEstimate(flops=cost, bytes_accessed=0, transcendentals=0),
        compiler_params=pltpu.CompilerParams(vmem_limit_bytes=limit),
    )(*args)


def frame(pos, corner):
    return corner[0] - pos[0] * ROWS, corner[1] - pos[1] * COLS


def corners(pos, local, lower, upper):
    moved = jnp.logical_and(lax.rem(pos[0], 2) == 0, lax.rem(pos[1], 2) == 1)
    local, lower, upper = frame(pos, local), frame(pos, lower), frame(pos, upper)
    here = tuple(jnp.where(moved, x, y) for x, y in zip(lower, local))
    up = tuple(jnp.where(moved, x, y) for x, y in zip(local, upper))
    return here, lower, up


def inside(rows, start):
    return jnp.logical_and(rows >= start, rows < start + M)


def pack_kernel(pos, local, lower, upper, spec, to_lower, to_upper):
    _, down, up = corners(pos, local, lower, upper)
    cols = lax.broadcasted_iota(jnp.int32, (ROWS, M), 1)
    for part in range(2):
        left = spec[part, :, :M]
        right = spec[part, :, M:]
        to_lower[part] = jnp.where(cols >= down[1], left, right)
        to_upper[part] = jnp.where(cols >= up[1], left, right)


def pupil_kernel(pos, local, lower, upper, pupil, rolled):
    (at_row, at_col), _, _ = corners(pos, local, lower, upper)
    shift = lax.rem(at_col, M)
    down = lax.rem(at_row + 2 * N, M)
    for part in range(2):
        rolled[part] = pltpu.roll(pltpu.roll(pupil[part], shift, 1), down, 0)[:ROWS]


def stage_kernel(spec, staged):
    staged[...] = spec[...]


def half_rows(table, half):
    where = pl.ds(pl.multiple_of(half * ROWS, ROWS), ROWS)
    return (table[0, where, :], table[1, where, :]), (table[2, where, :], table[3, where, :])


def half_cols(table, half):
    where = pl.ds(pl.multiple_of(half * ROWS, ROWS), ROWS)
    return (table[0, :, where], table[1, :, where]), (table[2, :, where], table[3, :, where])


def field_of(where, spec, from_lower, from_upper, pupil):
    (at_row, at_col), _, _ = corners(*where)
    cols = lax.broadcasted_iota(jnp.int32, (ROWS, M), 1)
    rows = lax.broadcasted_iota(jnp.int32, (ROWS, M), 0)
    field = []
    for part in range(2):
        own = jnp.where(cols >= at_col, spec[part, :, :M], spec[part, :, M:])
        other = jnp.where(inside(rows + M, at_row), from_upper[part], from_lower[part])
        field.append(jnp.where(inside(rows, at_row), own, other))
    re = split(pupil[0] * field[0] - pupil[1] * field[1])
    im = split(pupil[0] * field[1] + pupil[1] * field[0])
    return re, im


def send_kernel(pos, local, lower, upper, spec, from_lower, from_upper, pupil, table, send):
    re, im = field_of((pos, local, lower, upper), spec, from_lower, from_upper, pupil)
    cos, sin = half_cols(table, 1 - lax.rem(pos[0], 2))
    send[0], send[1] = complex_times_table(re, im, cos, sin, 1)


def keep_kernel(pos, local, lower, upper, spec, from_lower, from_upper, pupil, table, wave):
    parity = lax.rem(pos[0], 2)
    re, im = field_of((pos, local, lower, upper), spec, from_lower, from_upper, pupil)
    cos, sin = half_cols(table, parity)
    re, im = complex_times_table(re, im, cos, sin, 1)
    wave[0], wave[1] = table_times_complex(cos, sin, 1, split(re), split(im))


def fit_kernel(pos, far_amp, near_amp, amplitude, wave, other, table, fit, send):
    parity = lax.rem(pos[0], 2)
    moved = jnp.logical_and(parity == 0, lax.rem(pos[1], 2) == 1)
    cos, sin = half_cols(table, 1 - parity)
    wave_re, wave_im = table_times_complex(cos, sin, 1, split(other[0]), split(other[1]))
    wave_re += wave[0]
    wave_im += wave[1]
    measured = jnp.where(parity == 0, amplitude[:, :ROWS], amplitude[:, ROWS:])
    measured = jnp.where(moved, far_amp[...], measured) + near_amp[...]
    modulus = jnp.sqrt(wave_re * wave_re + wave_im * wave_im + GAMMA)
    keeping = 1.0 - measured / modulus
    fit[0] = wave_re * keeping
    fit[1] = wave_im * keeping
    cos, sin = half_rows(table, 1 - parity)
    send[0], send[1] = table_times_complex(cos, sin, -1, split(fit[0]), split(fit[1]))


def stay_kernel(pos, fit, table, part):
    cos, sin = half_rows(table, lax.rem(pos[0], 2))
    re, im = table_times_complex(cos, sin, -1, split(fit[0]), split(fit[1]))
    part[0], part[1] = complex_times_table(split(re), split(im), cos, sin, -1)


def grad_kernel(pos, part, other, pupil, table, grad):
    cos, sin = half_rows(table, 1 - lax.rem(pos[0], 2))
    re, im = complex_times_table(split(other[0]), split(other[1]), cos, sin, -1)
    re += part[0]
    im += part[1]
    back_re = pupil[0] * re + pupil[1] * im
    back_im = pupil[0] * im - pupil[1] * re
    for at, col in enumerate(ORDER):
        grad[at, 0] = back_re[col * LOW : col * LOW + LOW]
        grad[at, 1] = back_im[col * LOW : col * LOW + LOW]


def rows_kernel(pos, leds, own, lower_odd, upper_even, lower_even, upper_odd, twist, table, outgoing, shares, pencil, spectra, digits, sems):
    row, col = pos[0], pos[1]
    cols = lax.broadcasted_iota(jnp.int32, (LOW, M), 1)
    rows = lax.broadcasted_iota(jnp.int32, (LOW, M), 0) + col * LOW
    for at, source_col in enumerate(ORDER):
        lower, upper = (lower_even, upper_even) if at < 4 else (lower_odd, upper_odd)
        corner = [leds[source_col, index] for index in range(6)]
        around = corners((row, source_col), corner[:2], corner[2:4], corner[4:])
        for part in range(2):
            left = right = 0.0
            for (at_row, at_col), source in zip(around, (own[at, part], lower[at % 4, part], upper[at % 4, part])):
                value = jnp.where(inside(rows, at_row), source, 0.0)
                left = left + jnp.where(cols >= at_col, value, 0.0)
                right = right + jnp.where(cols < at_col, value, 0.0)
            pencil[source_col, part, :, :M] = left
            pencil[source_col, part, :, M:] = right
    copies = [
        pltpu.make_async_copy(
            pencil.at[source_col], shares.at[lax.rem(source_col - col + N_COL, N_COL)], sems.at[source_col]
        )
        for source_col in range(N_COL)
    ]
    for copy in copies:
        copy.start()
    for group in range(LOW // 8):
        for tile in range(2):
            lanes = slice(tile * 128, tile * 128 + 128)
            values = [
                tuple(
                    pencil[
                        at // 4,
                        part,
                        group * 8 : group * 8 + 8,
                        (at % 4) * 256 + tile * 128 : (at % 4) * 256 + tile * 128 + 128,
                    ]
                    for part in range(2)
                )
                for at in range(LOW)
            ]
            for at, (re, im) in enumerate(fft_list(values)):
                cos = twist[0, at : at + 1, lanes]
                sin = twist[1, at : at + 1, lanes]
                place = pl.ds((at // 8) * 256 + group * 64 + at % 8, 8, 8)
                digits[tile, place, :] = re * cos - im * sin
                digits[2 + tile, place, :] = re * sin + im * cos
    re = split(jnp.concatenate([digits[0], digits[1]], axis=1))
    im = split(jnp.concatenate([digits[2], digits[3]], axis=1))
    cos = (table[0], table[1])
    sin = (table[2], table[3])
    for part, flat in enumerate(complex_times_table(re, im, cos, sin, 1)):
        turned = flat.T
        for at in range(8):
            spectra[pl.ds(part * 8 + at, PARTS, 16), :] = turned[:, at * 128 : at * 128 + 128]
    last = pltpu.make_async_copy(spectra, outgoing, sems.at[N_COL])
    last.start()
    for copy in copies:
        copy.wait()
    last.wait()


def assemble_kernel(pos, *refs):
    total = refs[-1]
    for step, share in enumerate(refs[:-1]):
        where = pl.ds(pl.multiple_of(lax.rem(pos[1] - step + N_COL, N_COL) * LOW, LOW), LOW)
        for part in range(2):
            total[part, where, :] = share[part]


def final_kernel(incoming, twist, table, result, image, digits, sems):
    pair = []
    for part in range(2):
        flat = jnp.concatenate([incoming[pl.ds(part * 8 + at, PARTS, 16), :] for at in range(8)], axis=1)
        pair.append(split(flat.T))
    cos = (table[0], table[1])
    sin = (table[2], table[3])
    digits[0], digits[1] = complex_times_table(*pair, cos, sin, 1)
    copies = []
    for group in range(LOW // 8):
        for tile in range(2):
            lanes = slice(tile * 128, tile * 128 + 128)
            values = []
            for at in range(LOW):
                rows = slice(group * 256 + at * 8, group * 256 + at * 8 + 8)
                re = digits[0, rows, lanes]
                im = digits[1, rows, lanes]
                cos = twist[0, at : at + 1, lanes]
                sin = twist[1, at : at + 1, lanes]
                values.append((re * cos - im * sin, re * sin + im * cos))
            for at, value in enumerate(fft_list(values)):
                for part in range(2):
                    image[
                        part,
                        group * 8 : group * 8 + 8,
                        at * 256 + tile * 128 : at * 256 + tile * 128 + 128,
                    ] = value[part]
        rows = pl.ds(group * 8, 8)
        copies.append(pltpu.make_async_copy(image.at[:, rows], result.at[:, rows], sems.at[group]))
        copies[-1].start()
    for copy in copies:
        copy.wait()


def moves(rule):
    pairs = [(row, col, rule(row, col % 2)) for row in range(N_ROW) for col in range(N_COL)]
    return [(row * N_COL + col, to * N_COL + col) for row, col, to in pairs if to is not None]


def downward(row, core):
    return row - 2 if row >= 2 and (row % 2 == 1 or core == 0) else None


def upward(row, core):
    if row % 2 == 0:
        return (row + 2) % N_ROW if core == 1 else None
    return row + 2 if row + 2 < N_ROW else None


def partner(row, core):
    return row ^ 1 if core == 0 else (row + (1 if row % 2 == 1 else -1)) % N_ROW


def near(row, core):
    return row ^ 1 if core == 0 else (row + 1) % N_ROW


def far(row, core):
    return (row + 2) % N_ROW if core == 1 and row % 2 == 0 else None


BOTH = ("row", "col")
DOWN = moves(downward)
UP = moves(upward)
PARTNERS = moves(partner)
NEAR = moves(near)
FAR = moves(far)
FROM_LOWER = moves(lambda row, core: (row + 2) % N_ROW)
FROM_UPPER = moves(lambda row, core: row - 2 if row >= 2 and row % 2 == 1 else None)


def on_device(spectrum, pupil, amplitude, offsets, holds, window_table, part_table, twist):
    row = lax.axis_index("row")
    col = lax.axis_index("col")
    pos = jnp.stack([row, col]).astype(jnp.int32)
    local = offsets[0, 0]
    lower = lax.ppermute(local, BOTH, FROM_LOWER)
    upper = lax.ppermute(local, BOTH, FROM_UPPER)
    where = (pos, local, lower, upper)
    leds = lax.all_gather(jnp.concatenate([local, lower, upper]), "col")
    smem = (0, 1, 2, 3)
    measured = amplitude[0, 0]
    half = (ROWS, M)
    quarter = (2, ROWS, ROWS)
    near_half = lax.dynamic_slice(measured, (jnp.int32(0), (1 - row % 2) * ROWS), (M, ROWS))
    near_amp = lax.ppermute(near_half, BOTH, NEAR)
    far_amp = lax.ppermute(measured[:, :ROWS], BOTH, FAR)

    (staged,) = call(stage_kernel, [(2, ROWS, COLS)], (), spectrum, limit=4 * 1024 * 1024)()
    to_lower, to_upper = call(pack_kernel, [(2,) + half, (2,) + half], smem, *where, staged, limit=4 * 1024 * 1024)()
    from_upper = lax.ppermute(to_lower, BOTH, DOWN)
    from_lower = lax.ppermute(to_upper, BOTH, UP)
    (rolled,) = call(pupil_kernel, [(2,) + half], smem, *where, pupil)()

    sources = (*where, staged, from_lower, from_upper, rolled, window_table)
    (send,) = call(send_kernel, [quarter], smem, *sources)()
    other = lax.ppermute(send, BOTH, PARTNERS)
    (wave,) = call(keep_kernel, [(2, M, ROWS)], smem, *sources)()
    fit, send = call(
        fit_kernel, [(2, M, ROWS), quarter], (0,), pos, far_amp, near_amp, measured, wave, other, window_table
    )()
    other = lax.ppermute(send, BOTH, PARTNERS)
    (part,) = call(stay_kernel, [(2,) + half], (0,), pos, fit, window_table)()
    (grad,) = call(grad_kernel, [(N_COL, 2, LOW, M)], (0,), pos, part, other, rolled, window_table)()

    own = lax.all_to_all(grad, "col", split_axis=0, concat_axis=0, tiled=True, axis_index_groups=[ORDER])
    even, odd = own[:4], own[4:]
    lower_even = lax.ppermute(even, "row", [(row, row + 2) for row in range(N_ROW - 2)])
    upper_odd = lax.ppermute(odd, "row", [(row, row - 2) for row in range(2, N_ROW)] + [(0, N_ROW - 2)])
    lower_odd = lax.ppermute(odd, "row", [(row, row + 2) for row in range(1, N_ROW - 2, 2)])
    upper_even = lax.ppermute(even, "row", [(row, row - 2) for row in range(3, N_ROW, 2)])
    outgoing, shares = call(
        rows_kernel,
        [(PARTS * 16, 128), (N_COL, 2, LOW, COLS)],
        (0, 1),
        pos,
        leds,
        own,
        lower_odd,
        upper_even,
        lower_even,
        upper_odd,
        twist,
        part_table,
        hbm=True,
        limit=ROWS_VMEM_BYTES,
    )(
        [
            pltpu.VMEM((N_COL, 2, LOW, COLS), F32),
            pltpu.VMEM((PARTS * 16, 128), F32),
            pltpu.VMEM((4, COLS, 128), F32),
            pltpu.SemaphoreType.DMA((N_COL + 1,)),
        ]
    )
    back_shares = [shares[0]] + [
        lax.ppermute(shares[step], "col", [(at, (at + step) % N_COL) for at in range(N_COL)])
        for step in range(1, N_COL)
    ]
    (total,) = call(assemble_kernel, [(2, ROWS, COLS)], (0,), pos, *back_shares)()
    incoming = lax.all_to_all(
        outgoing.reshape(PARTS, 16, 128), ("row", "col"), split_axis=0, concat_axis=0, tiled=True
    ).reshape(PARTS * 16, 128)
    (image,) = call(final_kernel, [(2, LOW, N)], (), incoming, twist, part_table, hbm=True)(
        [pltpu.VMEM((2, LOW, N), F32), pltpu.VMEM((2, COLS, PARTS), F32), pltpu.SemaphoreType.DMA((LOW // 8,))]
    )
    return (total, image)


def solution(mesh):
    window_table = dft_tables(M, 1.0 / math.sqrt(M))
    part_table = dft_tables(PARTS, 1.0 / math.sqrt(N))
    twist = twist_tables()
    mapped = jax.shard_map(
        on_device,
        mesh=mesh,
        in_specs=(
            P(None, "row", "col"),
            P(),
            P("row", "col", None, None),
            P("row", "col", None),
            P("row", "col"),
            P(),
            P(),
            P(),
        ),
        out_specs=(P(None, "row", "col"), P(None, ("row", "col"), None)),
        check_vma=False,
    )

    def run(spectrum, pupil, amplitude, offsets, holds):
        return mapped(
            spectrum,
            pupil,
            amplitude,
            offsets,
            holds,
            jnp.asarray(window_table),
            jnp.asarray(part_table),
            jnp.asarray(twist),
        )

    return run
```

```python
import math

import jax
import jax.numpy as jnp
import ml_dtypes
import numpy as np
from jax import lax
from jax.experimental import pallas as pl
from jax.experimental.pallas import tpu as pltpu
from jax.sharding import PartitionSpec as P

GAMMA = 1.0
N = 8192
M = 512
ROWS = 256
COLS = 1024
N_ROW = 32
N_COL = 8
PARTS = N_ROW * N_COL
LOW = 32
ORDER = [0, 2, 4, 6, 1, 3, 5, 7]
F32 = jnp.float32
BF16 = jnp.bfloat16
VMEM_BYTES = 32 * 1024 * 1024
SLOW = 10**11
ROWS_VMEM_BYTES = 59 * 1024 * 1024


def halves(table):
    high = table.astype(np.float32).astype(ml_dtypes.bfloat16)
    low = (table - high.astype(np.float64)).astype(np.float32).astype(ml_dtypes.bfloat16)
    return high, low


def dft_tables(length, scale):
    counter = np.arange(length)
    angles = 2.0 * np.pi / length * (np.outer(counter, counter) % length)
    return np.stack(halves(np.cos(angles) * scale) + halves(np.sin(angles) * scale))


def twist_tables():
    angles = 2.0 * np.pi / N * np.outer(np.arange(LOW), np.arange(PARTS))
    return np.stack([np.cos(angles), np.sin(angles)]).astype(np.float32)


def split(values):
    high = values.astype(BF16)
    low = (values - high.astype(F32)).astype(BF16)
    return high, low


def mm(left, right):
    return jnp.dot(left, right, preferred_element_type=F32)


def six(first, second, axis):
    return jnp.concatenate([first[0], first[1], first[0], second[0], second[1], second[0]], axis=axis)


def six_table(first, second, axis):
    return jnp.concatenate([first[0], first[0], first[1], second[0], second[0], second[1]], axis=axis)


def minus(pair):
    return -pair[0], -pair[1]


def complex_times_table(re, im, cos, sin, sign):
    first, second = (minus(im), re) if sign > 0 else (im, minus(re))
    return (
        mm(six(re, first, 1), six_table(cos, sin, 0)),
        mm(six(second, im, 1), six_table(sin, cos, 0)),
    )


def table_times_complex(cos, sin, sign, re, im):
    first, second = (minus(im), re) if sign > 0 else (im, minus(re))
    return (
        mm(six_table(cos, sin, 1), six(re, first, 0)),
        mm(six_table(sin, cos, 1), six(second, im, 0)),
    )


def turn(value, numer, denom):
    re, im = value
    numer %= denom
    if numer == 0:
        return re, im
    if 4 * numer == denom:
        return -im, re
    if 2 * numer == denom:
        return -re, -im
    cos = math.cos(2.0 * math.pi * numer / denom)
    sin = math.sin(2.0 * math.pi * numer / denom)
    if 8 * numer == denom:
        return (re - im) * cos, (re + im) * cos
    if 8 * numer == 3 * denom:
        return (re + im) * -sin, (re - im) * sin
    return re * cos - im * sin, re * sin + im * cos


def fft_list(values):
    count = len(values)
    if count == 1:
        return values
    even = fft_list(values[0::2])
    odd = fft_list(values[1::2])
    first, second = [], []
    for at in range(count // 2):
        er, ei = even[at]
        tr, ti = turn(odd[at], at, count)
        first.append((er + tr, ei + ti))
        second.append((er - tr, ei - ti))
    return first + second


def call(kernel, outs, smem, *args, cost=None, hbm=False, limit=VMEM_BYTES):
    specs = [pl.BlockSpec(memory_space=pltpu.SMEM if at in smem else pltpu.VMEM) for at in range(len(args))]
    return lambda scratch=(): pl.pallas_call(
        kernel,
        out_shape=tuple(jax.ShapeDtypeStruct(shape, F32) for shape in outs),
        in_specs=specs,
        out_specs=tuple(pl.BlockSpec(memory_space=pltpu.HBM if hbm else pltpu.VMEM) for _ in outs),
        scratch_shapes=scratch,
        cost_estimate=cost and pl.CostEstimate(flops=cost, bytes_accessed=0, transcendentals=0),
        compiler_params=pltpu.CompilerParams(vmem_limit_bytes=limit),
    )(*args)


def frame(pos, corner):
    return corner[0] - pos[0] * ROWS, corner[1] - pos[1] * COLS


def corners(pos, local, lower, upper):
    moved = jnp.logical_and(lax.rem(pos[0], 2) == 0, lax.rem(pos[1], 2) == 1)
    local, lower, upper = frame(pos, local), frame(pos, lower), frame(pos, upper)
    here = tuple(jnp.where(moved, x, y) for x, y in zip(lower, local))
    up = tuple(jnp.where(moved, x, y) for x, y in zip(local, upper))
    return here, lower, up


def inside(rows, start):
    return jnp.logical_and(rows >= start, rows < start + M)


def pack_kernel(pos, local, lower, upper, spec, to_lower, to_upper):
    _, down, up = corners(pos, local, lower, upper)
    cols = lax.broadcasted_iota(jnp.int32, (ROWS, M), 1)
    for part in range(2):
        left = spec[part, :, :M]
        right = spec[part, :, M:]
        to_lower[part] = jnp.where(cols >= down[1], left, right)
        to_upper[part] = jnp.where(cols >= up[1], left, right)


def pupil_kernel(pos, local, lower, upper, pupil, amplitude, near_amp, rolled, measured, far_half):
    (at_row, at_col), _, _ = corners(pos, local, lower, upper)
    shift = lax.rem(at_col, M)
    down = lax.rem(at_row + 2 * N, M)
    for part in range(2):
        rolled[part] = pltpu.roll(pltpu.roll(pupil[part], shift, 1), down, 0)[:ROWS]
    low = lax.rem(pos[0], 2) == 0
    moved = jnp.logical_and(low, lax.rem(pos[1], 2) == 1)
    own = jnp.where(low, amplitude[:, :ROWS], amplitude[:, ROWS:])
    measured[...] = jnp.where(moved, 0.0, own) + near_amp[...]
    far_half[...] = amplitude[:, :ROWS]


def stage_kernel(spec, staged):
    staged[...] = spec[...]


def half_rows(table, half):
    where = pl.ds(pl.multiple_of(half * ROWS, ROWS), ROWS)
    return (table[0, where, :], table[1, where, :]), (table[2, where, :], table[3, where, :])


def half_cols(table, half):
    where = pl.ds(pl.multiple_of(half * ROWS, ROWS), ROWS)
    return (table[0, :, where], table[1, :, where]), (table[2, :, where], table[3, :, where])


def field_of(where, spec, from_lower, from_upper, pupil):
    (at_row, at_col), _, _ = corners(*where)
    cols = lax.broadcasted_iota(jnp.int32, (ROWS, M), 1)
    rows = lax.broadcasted_iota(jnp.int32, (ROWS, M), 0)
    field = []
    for part in range(2):
        own = jnp.where(cols >= at_col, spec[part, :, :M], spec[part, :, M:])
        other = jnp.where(inside(rows + M, at_row), from_upper[part], from_lower[part])
        field.append(jnp.where(inside(rows, at_row), own, other))
    re = split(pupil[0] * field[0] - pupil[1] * field[1])
    im = split(pupil[0] * field[1] + pupil[1] * field[0])
    return re, im


def send_kernel(pos, local, lower, upper, spec, from_lower, from_upper, pupil, table, send):
    re, im = field_of((pos, local, lower, upper), spec, from_lower, from_upper, pupil)
    cos, sin = half_cols(table, 1 - lax.rem(pos[0], 2))
    send[0], send[1] = complex_times_table(re, im, cos, sin, 1)


def keep_kernel(pos, local, lower, upper, spec, from_lower, from_upper, pupil, table, wave):
    parity = lax.rem(pos[0], 2)
    re, im = field_of((pos, local, lower, upper), spec, from_lower, from_upper, pupil)
    cos, sin = half_cols(table, parity)
    re, im = complex_times_table(re, im, cos, sin, 1)
    wave[0], wave[1] = table_times_complex(cos, sin, 1, split(re), split(im))


def fit_kernel(pos, far_amp, measured, wave, other, table, fit, send):
    parity = lax.rem(pos[0], 2)
    cos, sin = half_cols(table, 1 - parity)
    wave_re, wave_im = table_times_complex(cos, sin, 1, split(other[0]), split(other[1]))
    wave_re += wave[0]
    wave_im += wave[1]
    modulus = jnp.sqrt(wave_re * wave_re + wave_im * wave_im + GAMMA)
    keeping = 1.0 - (measured[...] + far_amp[...]) / modulus
    fit[0] = wave_re * keeping
    fit[1] = wave_im * keeping
    cos, sin = half_rows(table, 1 - parity)
    send[0], send[1] = table_times_complex(cos, sin, -1, split(fit[0]), split(fit[1]))


def stay_kernel(pos, fit, table, part):
    cos, sin = half_rows(table, lax.rem(pos[0], 2))
    re, im = table_times_complex(cos, sin, -1, split(fit[0]), split(fit[1]))
    part[0], part[1] = complex_times_table(split(re), split(im), cos, sin, -1)


def grad_kernel(pos, part, other, pupil, table, grad):
    cos, sin = half_rows(table, 1 - lax.rem(pos[0], 2))
    re, im = complex_times_table(split(other[0]), split(other[1]), cos, sin, -1)
    re += part[0]
    im += part[1]
    back_re = pupil[0] * re + pupil[1] * im
    back_im = pupil[0] * im - pupil[1] * re
    for at, col in enumerate(ORDER):
        grad[at, 0] = back_re[col * LOW : col * LOW + LOW]
        grad[at, 1] = back_im[col * LOW : col * LOW + LOW]


def rows_kernel(pos, leds, own, lower_odd, upper_even, lower_even, upper_odd, twist, table, outgoing, shares, pencil, spectra, digits, sems):
    row, col = pos[0], pos[1]
    cols = lax.broadcasted_iota(jnp.int32, (LOW, M), 1)
    rows = lax.broadcasted_iota(jnp.int32, (LOW, M), 0) + col * LOW
    for at, source_col in enumerate(ORDER):
        lower, upper = (lower_even, upper_even) if at < 4 else (lower_odd, upper_odd)
        corner = [leds[source_col, index] for index in range(6)]
        around = corners((row, source_col), corner[:2], corner[2:4], corner[4:])
        for part in range(2):
            left = right = 0.0
            for (at_row, at_col), source in zip(around, (own[at, part], lower[at % 4, part], upper[at % 4, part])):
                value = jnp.where(inside(rows, at_row), source, 0.0)
                left = left + jnp.where(cols >= at_col, value, 0.0)
                right = right + jnp.where(cols < at_col, value, 0.0)
            pencil[source_col, part, :, :M] = left
            pencil[source_col, part, :, M:] = right
    copies = [
        pltpu.make_async_copy(
            pencil.at[source_col], shares.at[lax.rem(source_col - col + N_COL, N_COL)], sems.at[source_col]
        )
        for source_col in range(N_COL)
    ]
    for copy in copies:
        copy.start()
    for group in range(LOW // 8):
        for tile in range(2):
            lanes = slice(tile * 128, tile * 128 + 128)
            values = [
                tuple(
                    pencil[
                        at // 4,
                        part,
                        group * 8 : group * 8 + 8,
                        (at % 4) * 256 + tile * 128 : (at % 4) * 256 + tile * 128 + 128,
                    ]
                    for part in range(2)
                )
                for at in range(LOW)
            ]
            for at, (re, im) in enumerate(fft_list(values)):
                cos = twist[0, at : at + 1, lanes]
                sin = twist[1, at : at + 1, lanes]
                place = pl.ds((at // 8) * 256 + group * 64 + at % 8, 8, 8)
                digits[tile, place, :] = re * cos - im * sin
                digits[2 + tile, place, :] = re * sin + im * cos
    re = split(jnp.concatenate([digits[0], digits[1]], axis=1))
    im = split(jnp.concatenate([digits[2], digits[3]], axis=1))
    cos = (table[0], table[1])
    sin = (table[2], table[3])
    for part, flat in enumerate(complex_times_table(re, im, cos, sin, 1)):
        turned = flat.T
        for at in range(8):
            spectra[pl.ds(part * 8 + at, PARTS, 16), :] = turned[:, at * 128 : at * 128 + 128]
    last = pltpu.make_async_copy(spectra, outgoing, sems.at[N_COL])
    last.start()
    for copy in copies:
        copy.wait()
    last.wait()


def assemble_kernel(pos, *refs):
    total = refs[-1]
    for step, share in enumerate(refs[:-1]):
        where = pl.ds(pl.multiple_of(lax.rem(pos[1] - step + N_COL, N_COL) * LOW, LOW), LOW)
        for part in range(2):
            total[part, where, :] = share[part]


def final_kernel(incoming, twist, table, result, image, digits, sems):
    pair = []
    for part in range(2):
        flat = jnp.concatenate([incoming[pl.ds(part * 8 + at, PARTS, 16), :] for at in range(8)], axis=1)
        pair.append(split(flat.T))
    cos = (table[0], table[1])
    sin = (table[2], table[3])
    digits[0], digits[1] = complex_times_table(*pair, cos, sin, 1)
    copies = []
    for group in range(LOW // 8):
        for tile in range(2):
            lanes = slice(tile * 128, tile * 128 + 128)
            values = []
            for at in range(LOW):
                rows = slice(group * 256 + at * 8, group * 256 + at * 8 + 8)
                re = digits[0, rows, lanes]
                im = digits[1, rows, lanes]
                cos = twist[0, at : at + 1, lanes]
                sin = twist[1, at : at + 1, lanes]
                values.append((re * cos - im * sin, re * sin + im * cos))
            for at, value in enumerate(fft_list(values)):
                for part in range(2):
                    image[
                        part,
                        group * 8 : group * 8 + 8,
                        at * 256 + tile * 128 : at * 256 + tile * 128 + 128,
                    ] = value[part]
        rows = pl.ds(group * 8, 8)
        copies.append(pltpu.make_async_copy(image.at[:, rows], result.at[:, rows], sems.at[group]))
        copies[-1].start()
    for copy in copies:
        copy.wait()


def moves(rule):
    pairs = [(row, col, rule(row, col % 2)) for row in range(N_ROW) for col in range(N_COL)]
    return [(row * N_COL + col, to * N_COL + col) for row, col, to in pairs if to is not None]


def downward(row, core):
    return row - 2 if row >= 2 and (row % 2 == 1 or core == 0) else None


def upward(row, core):
    if row % 2 == 0:
        return (row + 2) % N_ROW if core == 1 else None
    return row + 2 if row + 2 < N_ROW else None


def partner(row, core):
    return row ^ 1 if core == 0 else (row + (1 if row % 2 == 1 else -1)) % N_ROW


def near(row, core):
    return row ^ 1 if core == 0 else (row + 1) % N_ROW


def far(row, core):
    return (row + 2) % N_ROW if core == 1 and row % 2 == 0 else None


BOTH = ("row", "col")
DOWN = moves(downward)
UP = moves(upward)
PARTNERS = moves(partner)
NEAR = moves(near)
FAR = moves(far)
FROM_LOWER = moves(lambda row, core: (row + 2) % N_ROW)
FROM_UPPER = moves(lambda row, core: row - 2 if row >= 2 and row % 2 == 1 else None)


def on_device(spectrum, pupil, amplitude, offsets, holds, window_table, part_table, twist):
    row = lax.axis_index("row")
    col = lax.axis_index("col")
    pos = jnp.stack([row, col]).astype(jnp.int32)
    local = offsets[0, 0]
    lower = lax.ppermute(local, BOTH, FROM_LOWER)
    upper = lax.ppermute(local, BOTH, FROM_UPPER)
    where = (pos, local, lower, upper)
    leds = lax.all_gather(jnp.concatenate([local, lower, upper]), "col")
    smem = (0, 1, 2, 3)
    measured = amplitude[0, 0]
    half = (ROWS, M)
    quarter = (2, ROWS, ROWS)
    near_half = lax.dynamic_slice(measured, (jnp.int32(0), (1 - row % 2) * ROWS), (M, ROWS))
    near_amp = lax.ppermute(near_half, BOTH, NEAR)

    (staged,) = call(stage_kernel, [(2, ROWS, COLS)], (), spectrum, limit=4 * 1024 * 1024)()
    to_lower, to_upper = call(pack_kernel, [(2,) + half, (2,) + half], smem, *where, staged, cost=SLOW, limit=4 * 1024 * 1024)()
    from_upper = lax.ppermute(to_lower, BOTH, DOWN)
    from_lower = lax.ppermute(to_upper, BOTH, UP)
    rolled, measured, far_half = call(
        pupil_kernel, [(2,) + half, (M, ROWS), (M, ROWS)], smem, *where, pupil, measured, near_amp, cost=SLOW
    )()
    far_amp = lax.ppermute(far_half, BOTH, FAR)

    sources = (*where, staged, from_lower, from_upper, rolled, window_table)
    (send,) = call(send_kernel, [quarter], smem, *sources)()
    other = lax.ppermute(send, BOTH, PARTNERS)
    (wave,) = call(keep_kernel, [(2, M, ROWS)], smem, *sources)()
    fit, send = call(
        fit_kernel, [(2, M, ROWS), quarter], (0,), pos, far_amp, measured, wave, other, window_table
    )()
    other = lax.ppermute(send, BOTH, PARTNERS)
    (part,) = call(stay_kernel, [(2,) + half], (0,), pos, fit, window_table)()
    (grad,) = call(grad_kernel, [(N_COL, 2, LOW, M)], (0,), pos, part, other, rolled, window_table)()

    own = lax.all_to_all(grad, "col", split_axis=0, concat_axis=0, tiled=True, axis_index_groups=[ORDER])
    even, odd = own[:4], own[4:]
    lower_even = lax.ppermute(even, "row", [(row, row + 2) for row in range(N_ROW - 2)])
    upper_odd = lax.ppermute(odd, "row", [(row, row - 2) for row in range(2, N_ROW)] + [(0, N_ROW - 2)])
    lower_odd = lax.ppermute(odd, "row", [(row, row + 2) for row in range(1, N_ROW - 2, 2)])
    upper_even = lax.ppermute(even, "row", [(row, row - 2) for row in range(3, N_ROW, 2)])
    outgoing, shares = call(
        rows_kernel,
        [(PARTS * 16, 128), (N_COL, 2, LOW, COLS)],
        (0, 1),
        pos,
        leds,
        own,
        lower_odd,
        upper_even,
        lower_even,
        upper_odd,
        twist,
        part_table,
        hbm=True,
        limit=ROWS_VMEM_BYTES,
    )(
        [
            pltpu.VMEM((N_COL, 2, LOW, COLS), F32),
            pltpu.VMEM((PARTS * 16, 128), F32),
            pltpu.VMEM((4, COLS, 128), F32),
            pltpu.SemaphoreType.DMA((N_COL + 1,)),
        ]
    )
    back_shares = [shares[0]] + [
        lax.ppermute(shares[step], "col", [(at, (at + step) % N_COL) for at in range(N_COL)])
        for step in range(1, N_COL)
    ]
    (total,) = call(assemble_kernel, [(2, ROWS, COLS)], (0,), pos, *back_shares)()
    incoming = lax.all_to_all(
        outgoing.reshape(PARTS, 16, 128), ("row", "col"), split_axis=0, concat_axis=0, tiled=True
    ).reshape(PARTS * 16, 128)
    (image,) = call(final_kernel, [(2, LOW, N)], (), incoming, twist, part_table, hbm=True)(
        [pltpu.VMEM((2, LOW, N), F32), pltpu.VMEM((2, COLS, PARTS), F32), pltpu.SemaphoreType.DMA((LOW // 8,))]
    )
    return (total, image)


def solution(mesh):
    window_table = dft_tables(M, 1.0 / math.sqrt(M))
    part_table = dft_tables(PARTS, 1.0 / math.sqrt(N))
    twist = twist_tables()
    mapped = jax.shard_map(
        on_device,
        mesh=mesh,
        in_specs=(
            P(None, "row", "col"),
            P(),
            P("row", "col", None, None),
            P("row", "col", None),
            P("row", "col"),
            P(),
            P(),
            P(),
        ),
        out_specs=(P(None, "row", "col"), P(None, ("row", "col"), None)),
        check_vma=False,
    )

    def run(spectrum, pupil, amplitude, offsets, holds):
        return mapped(
            spectrum,
            pupil,
            amplitude,
            offsets,
            holds,
            jnp.asarray(window_table),
            jnp.asarray(part_table),
            jnp.asarray(twist),
        )

    return run
```

```python
import math

import jax
import jax.numpy as jnp
import ml_dtypes
import numpy as np
from jax import lax
from jax.experimental import pallas as pl
from jax.experimental.pallas import tpu as pltpu
from jax.sharding import PartitionSpec as P

GAMMA = 1.0
N = 8192
M = 512
ROWS = 256
COLS = 1024
N_ROW = 32
N_COL = 8
PARTS = N_ROW * N_COL
LOW = 32
RING = 8
ORDER = [0, 2, 4, 6, 1, 3, 5, 7]
F32 = jnp.float32
BF16 = jnp.bfloat16
VMEM_BYTES = 32 * 1024 * 1024
SLOW = 10**11
ROWS_VMEM_BYTES = 59 * 1024 * 1024


def halves(table):
    high = table.astype(np.float32).astype(ml_dtypes.bfloat16)
    low = (table - high.astype(np.float64)).astype(np.float32).astype(ml_dtypes.bfloat16)
    return high, low


def dft_tables(length, scale):
    counter = np.arange(length)
    angles = 2.0 * np.pi / length * (np.outer(counter, counter) % length)
    return np.stack(halves(np.cos(angles) * scale) + halves(np.sin(angles) * scale))


def twist_tables():
    angles = 2.0 * np.pi / N * np.outer(np.arange(LOW), np.arange(PARTS))
    return np.stack([np.cos(angles), np.sin(angles)]).astype(np.float32)


def split(values):
    high = values.astype(BF16)
    low = (values - high.astype(F32)).astype(BF16)
    return high, low


def mm(left, right):
    return jnp.dot(left, right, preferred_element_type=F32)


def six(first, second, axis):
    return jnp.concatenate([first[0], first[1], first[0], second[0], second[1], second[0]], axis=axis)


def six_table(first, second, axis):
    return jnp.concatenate([first[0], first[0], first[1], second[0], second[0], second[1]], axis=axis)


def minus(pair):
    return -pair[0], -pair[1]


def complex_times_table(re, im, cos, sin, sign):
    first, second = (minus(im), re) if sign > 0 else (im, minus(re))
    return (
        mm(six(re, first, 1), six_table(cos, sin, 0)),
        mm(six(second, im, 1), six_table(sin, cos, 0)),
    )


def table_times_complex(cos, sin, sign, re, im):
    first, second = (minus(im), re) if sign > 0 else (im, minus(re))
    return (
        mm(six_table(cos, sin, 1), six(re, first, 0)),
        mm(six_table(sin, cos, 1), six(second, im, 0)),
    )


def turn(value, numer, denom):
    re, im = value
    numer %= denom
    if numer == 0:
        return re, im
    if 4 * numer == denom:
        return -im, re
    if 2 * numer == denom:
        return -re, -im
    cos = math.cos(2.0 * math.pi * numer / denom)
    sin = math.sin(2.0 * math.pi * numer / denom)
    if 8 * numer == denom:
        return (re - im) * cos, (re + im) * cos
    if 8 * numer == 3 * denom:
        return (re + im) * -sin, (re - im) * sin
    return re * cos - im * sin, re * sin + im * cos


def fft_list(values):
    count = len(values)
    if count == 1:
        return values
    even = fft_list(values[0::2])
    odd = fft_list(values[1::2])
    first, second = [], []
    for at in range(count // 2):
        er, ei = even[at]
        tr, ti = turn(odd[at], at, count)
        first.append((er + tr, ei + ti))
        second.append((er - tr, ei - ti))
    return first + second


def call(kernel, outs, smem, *args, cost=None, hbm=False, limit=VMEM_BYTES):
    specs = [pl.BlockSpec(memory_space=pltpu.SMEM if at in smem else pltpu.VMEM) for at in range(len(args))]
    return lambda scratch=(): pl.pallas_call(
        kernel,
        out_shape=tuple(jax.ShapeDtypeStruct(shape, F32) for shape in outs),
        in_specs=specs,
        out_specs=tuple(pl.BlockSpec(memory_space=pltpu.HBM if hbm else pltpu.VMEM) for _ in outs),
        scratch_shapes=scratch,
        cost_estimate=cost and pl.CostEstimate(flops=cost, bytes_accessed=0, transcendentals=0),
        compiler_params=pltpu.CompilerParams(vmem_limit_bytes=limit),
    )(*args)


def frame(pos, corner):
    return corner[0] - pos[0] * ROWS, corner[1] - pos[1] * COLS


def corners(pos, local, lower, upper):
    moved = jnp.logical_and(lax.rem(pos[0], 2) == 0, lax.rem(pos[1], 2) == 1)
    first = lax.rem(pos[0], RING) == 0
    local, lower, upper = frame(pos, local), frame(pos, lower), frame(pos, upper)
    shared = tuple(jnp.where(first, x, y) for x, y in zip(upper, lower))
    here = tuple(jnp.where(moved, x, y) for x, y in zip(shared, local))
    up = tuple(jnp.where(moved, x, y) for x, y in zip(local, upper))
    return here, lower, up


def inside(rows, start):
    return jnp.logical_and(rows >= start, rows < start + M)


def pack_kernel(pos, local, lower, upper, spec, to_lower, to_upper):
    _, down, up = corners(pos, local, lower, upper)
    cols = lax.broadcasted_iota(jnp.int32, (ROWS, M), 1)
    for part in range(2):
        left = spec[part, :, :M]
        right = spec[part, :, M:]
        to_lower[part] = jnp.where(cols >= down[1], left, right)
        to_upper[part] = jnp.where(cols >= up[1], left, right)


def pupil_kernel(pos, local, lower, upper, pupil, amplitude, near_amp, rolled, measured, far_half):
    (at_row, at_col), _, _ = corners(pos, local, lower, upper)
    shift = lax.rem(at_col, M)
    down = lax.rem(at_row + 2 * N, M)
    for part in range(2):
        rolled[part] = pltpu.roll(pltpu.roll(pupil[part], shift, 1), down, 0)[:ROWS]
    low = lax.rem(pos[0], 2) == 0
    moved = jnp.logical_and(low, lax.rem(pos[1], 2) == 1)
    own = jnp.where(low, amplitude[:, :ROWS], amplitude[:, ROWS:])
    measured[...] = jnp.where(moved, 0.0, own) + near_amp[...]
    far_half[...] = amplitude[:, :ROWS]


def stage_kernel(spec, staged):
    staged[...] = spec[...]


def half_rows(table, half):
    where = pl.ds(pl.multiple_of(half * ROWS, ROWS), ROWS)
    return (table[0, where, :], table[1, where, :]), (table[2, where, :], table[3, where, :])


def half_cols(table, half):
    where = pl.ds(pl.multiple_of(half * ROWS, ROWS), ROWS)
    return (table[0, :, where], table[1, :, where]), (table[2, :, where], table[3, :, where])


def field_of(where, spec, from_lower, from_upper, pupil):
    (at_row, at_col), _, _ = corners(*where)
    row, col = where[0][0], where[0][1]
    around = jnp.logical_and(lax.rem(row, RING) == 0, lax.rem(col, 2) == 1)
    ahead = jnp.where(around, RING * ROWS, M)
    cols = lax.broadcasted_iota(jnp.int32, (ROWS, M), 1)
    rows = lax.broadcasted_iota(jnp.int32, (ROWS, M), 0)
    field = []
    for part in range(2):
        own = jnp.where(cols >= at_col, spec[part, :, :M], spec[part, :, M:])
        other = jnp.where(inside(rows + ahead, at_row), from_upper[part], from_lower[part])
        field.append(jnp.where(inside(rows, at_row), own, other))
    re = split(pupil[0] * field[0] - pupil[1] * field[1])
    im = split(pupil[0] * field[1] + pupil[1] * field[0])
    return re, im


def send_kernel(pos, local, lower, upper, spec, from_lower, from_upper, pupil, table, send):
    re, im = field_of((pos, local, lower, upper), spec, from_lower, from_upper, pupil)
    cos, sin = half_cols(table, 1 - lax.rem(pos[0], 2))
    send[0], send[1] = complex_times_table(re, im, cos, sin, 1)


def keep_kernel(pos, local, lower, upper, spec, from_lower, from_upper, pupil, table, wave):
    parity = lax.rem(pos[0], 2)
    re, im = field_of((pos, local, lower, upper), spec, from_lower, from_upper, pupil)
    cos, sin = half_cols(table, parity)
    re, im = complex_times_table(re, im, cos, sin, 1)
    wave[0], wave[1] = table_times_complex(cos, sin, 1, split(re), split(im))


def fit_kernel(pos, far_amp, measured, wave, other, table, fit, send):
    parity = lax.rem(pos[0], 2)
    cos, sin = half_cols(table, 1 - parity)
    wave_re, wave_im = table_times_complex(cos, sin, 1, split(other[0]), split(other[1]))
    wave_re += wave[0]
    wave_im += wave[1]
    modulus = jnp.sqrt(wave_re * wave_re + wave_im * wave_im + GAMMA)
    keeping = 1.0 - (measured[...] + far_amp[...]) / modulus
    fit[0] = wave_re * keeping
    fit[1] = wave_im * keeping
    cos, sin = half_rows(table, 1 - parity)
    send[0], send[1] = table_times_complex(cos, sin, -1, split(fit[0]), split(fit[1]))


def stay_kernel(pos, fit, table, part):
    cos, sin = half_rows(table, lax.rem(pos[0], 2))
    re, im = table_times_complex(cos, sin, -1, split(fit[0]), split(fit[1]))
    part[0], part[1] = complex_times_table(split(re), split(im), cos, sin, -1)


def grad_kernel(pos, part, other, pupil, table, grad):
    cos, sin = half_rows(table, 1 - lax.rem(pos[0], 2))
    re, im = complex_times_table(split(other[0]), split(other[1]), cos, sin, -1)
    re += part[0]
    im += part[1]
    back_re = pupil[0] * re + pupil[1] * im
    back_im = pupil[0] * im - pupil[1] * re
    for at, col in enumerate(ORDER):
        grad[at, 0] = back_re[col * LOW : col * LOW + LOW]
        grad[at, 1] = back_im[col * LOW : col * LOW + LOW]


def rows_kernel(pos, leds, own, lower_odd, upper_even, lower_even, upper_odd, twist, table, outgoing, shares, pencil, spectra, digits, sems):
    row, col = pos[0], pos[1]
    cols = lax.broadcasted_iota(jnp.int32, (LOW, M), 1)
    rows = lax.broadcasted_iota(jnp.int32, (LOW, M), 0) + col * LOW
    for at, source_col in enumerate(ORDER):
        lower, upper = (lower_even, upper_even) if at < 4 else (lower_odd, upper_odd)
        corner = [leds[source_col, index] for index in range(6)]
        around = corners((row, source_col), corner[:2], corner[2:4], corner[4:])
        for part in range(2):
            left = right = 0.0
            for (at_row, at_col), source in zip(around, (own[at, part], lower[at % 4, part], upper[at % 4, part])):
                value = jnp.where(inside(rows, at_row), source, 0.0)
                left = left + jnp.where(cols >= at_col, value, 0.0)
                right = right + jnp.where(cols < at_col, value, 0.0)
            pencil[source_col, part, :, :M] = left
            pencil[source_col, part, :, M:] = right
    copies = [
        pltpu.make_async_copy(
            pencil.at[source_col], shares.at[lax.rem(source_col - col + N_COL, N_COL)], sems.at[source_col]
        )
        for source_col in range(N_COL)
    ]
    for copy in copies:
        copy.start()
    for group in range(LOW // 8):
        for tile in range(2):
            lanes = slice(tile * 128, tile * 128 + 128)
            values = [
                tuple(
                    pencil[
                        at // 4,
                        part,
                        group * 8 : group * 8 + 8,
                        (at % 4) * 256 + tile * 128 : (at % 4) * 256 + tile * 128 + 128,
                    ]
                    for part in range(2)
                )
                for at in range(LOW)
            ]
            for at, (re, im) in enumerate(fft_list(values)):
                cos = twist[0, at : at + 1, lanes]
                sin = twist[1, at : at + 1, lanes]
                place = pl.ds((at // 8) * 256 + group * 64 + at % 8, 8, 8)
                digits[tile, place, :] = re * cos - im * sin
                digits[2 + tile, place, :] = re * sin + im * cos
    re = split(jnp.concatenate([digits[0], digits[1]], axis=1))
    im = split(jnp.concatenate([digits[2], digits[3]], axis=1))
    cos = (table[0], table[1])
    sin = (table[2], table[3])
    for part, flat in enumerate(complex_times_table(re, im, cos, sin, 1)):
        turned = flat.T
        for at in range(8):
            spectra[pl.ds(part * 8 + at, PARTS, 16), :] = turned[:, at * 128 : at * 128 + 128]
    last = pltpu.make_async_copy(spectra, outgoing, sems.at[N_COL])
    last.start()
    for copy in copies:
        copy.wait()
    last.wait()


def assemble_kernel(pos, *refs):
    total = refs[-1]
    for step, share in enumerate(refs[:-1]):
        where = pl.ds(pl.multiple_of(lax.rem(pos[1] - step + N_COL, N_COL) * LOW, LOW), LOW)
        for part in range(2):
            total[part, where, :] = share[part]


def final_kernel(incoming, twist, table, result, image, digits, sems):
    pair = []
    for part in range(2):
        flat = jnp.concatenate([incoming[pl.ds(part * 8 + at, PARTS, 16), :] for at in range(8)], axis=1)
        pair.append(split(flat.T))
    cos = (table[0], table[1])
    sin = (table[2], table[3])
    digits[0], digits[1] = complex_times_table(*pair, cos, sin, 1)
    copies = []
    for group in range(LOW // 8):
        for tile in range(2):
            lanes = slice(tile * 128, tile * 128 + 128)
            values = []
            for at in range(LOW):
                rows = slice(group * 256 + at * 8, group * 256 + at * 8 + 8)
                re = digits[0, rows, lanes]
                im = digits[1, rows, lanes]
                cos = twist[0, at : at + 1, lanes]
                sin = twist[1, at : at + 1, lanes]
                values.append((re * cos - im * sin, re * sin + im * cos))
            for at, value in enumerate(fft_list(values)):
                for part in range(2):
                    image[
                        part,
                        group * 8 : group * 8 + 8,
                        at * 256 + tile * 128 : at * 256 + tile * 128 + 128,
                    ] = value[part]
        rows = pl.ds(group * 8, 8)
        copies.append(pltpu.make_async_copy(image.at[:, rows], result.at[:, rows], sems.at[group]))
        copies[-1].start()
    for copy in copies:
        copy.wait()


def moves(rule):
    pairs = [(row, col, rule(row, col % 2)) for row in range(N_ROW) for col in range(N_COL)]
    return [(row * N_COL + col, to * N_COL + col) for row, col, to in pairs if to is not None]


def downward(row, core):
    if row % RING == 0 and core == 1:
        return row - RING if row >= RING else None
    return row - 2 if row >= 2 and (row % 2 == 1 or core == 0) else None


def second(row):
    return row + 2 if row % RING < RING - 2 else row - (RING - 2)


def upward(row, core):
    if row % 2 == 0:
        return second(row) if core == 1 else None
    return row + 2 if row + 2 < N_ROW else None


def ring_step(row, by):
    return row // RING * RING + (row + by) % RING


def partner(row, core):
    return row ^ 1 if core == 0 else ring_step(row, 1 if row % 2 == 1 else -1)


def near(row, core):
    return row ^ 1 if core == 0 else ring_step(row, 1)


def far(row, core):
    return second(row) if core == 1 and row % 2 == 0 else None


def from_upper_row(row, core):
    return second(row) if core == 1 and row % 2 == 0 else (row - 2) % N_ROW


BOTH = ("row", "col")
DOWN = moves(downward)
UP = moves(upward)
PARTNERS = moves(partner)
NEAR = moves(near)
FAR = moves(far)
FROM_LOWER = moves(lambda row, core: (row + 2) % N_ROW)
FROM_UPPER = moves(from_upper_row)


def on_device(spectrum, pupil, amplitude, offsets, holds, window_table, part_table, twist):
    row = lax.axis_index("row")
    col = lax.axis_index("col")
    pos = jnp.stack([row, col]).astype(jnp.int32)
    local = offsets[0, 0]
    lower = lax.ppermute(local, BOTH, FROM_LOWER)
    upper = lax.ppermute(local, BOTH, FROM_UPPER)
    where = (pos, local, lower, upper)
    leds = lax.all_gather(jnp.concatenate([local, lower, upper]), "col")
    smem = (0, 1, 2, 3)
    measured = amplitude[0, 0]
    half = (ROWS, M)
    quarter = (2, ROWS, ROWS)
    near_half = lax.dynamic_slice(measured, (jnp.int32(0), (1 - row % 2) * ROWS), (M, ROWS))
    near_amp = lax.ppermute(near_half, BOTH, NEAR)

    (staged,) = call(stage_kernel, [(2, ROWS, COLS)], (), spectrum, limit=4 * 1024 * 1024)()
    to_lower, to_upper = call(pack_kernel, [(2,) + half, (2,) + half], smem, *where, staged, cost=SLOW, limit=4 * 1024 * 1024)()
    from_upper = lax.ppermute(to_lower, BOTH, DOWN)
    from_lower = lax.ppermute(to_upper, BOTH, UP)
    rolled, measured, far_half = call(
        pupil_kernel, [(2,) + half, (M, ROWS), (M, ROWS)], smem, *where, pupil, measured, near_amp, cost=SLOW
    )()
    far_amp = lax.ppermute(far_half, BOTH, FAR)

    sources = (*where, staged, from_lower, from_upper, rolled, window_table)
    (send,) = call(send_kernel, [quarter], smem, *sources)()
    other = lax.ppermute(send, BOTH, PARTNERS)
    (wave,) = call(keep_kernel, [(2, M, ROWS)], smem, *sources)()
    fit, send = call(
        fit_kernel, [(2, M, ROWS), quarter], (0,), pos, far_amp, measured, wave, other, window_table
    )()
    other = lax.ppermute(send, BOTH, PARTNERS)
    (part,) = call(stay_kernel, [(2,) + half], (0,), pos, fit, window_table)()
    (grad,) = call(grad_kernel, [(N_COL, 2, LOW, M)], (0,), pos, part, other, rolled, window_table)()

    own = lax.all_to_all(grad, "col", split_axis=0, concat_axis=0, tiled=True, axis_index_groups=[ORDER])
    even, odd = own[:4], own[4:]
    lower_even = lax.ppermute(even, "row", [(row, row + 2) for row in range(N_ROW - 2)])
    upper_odd = lax.ppermute(odd, "row", [(row, row + RING - 2 if row % RING == 0 else row - 2) for row in range(N_ROW) if row != 1])
    ahead = [(row, row + RING) for row in range(0, N_ROW - RING, RING)]
    lower_odd = lax.ppermute(odd, "row", [(row, row + 2) for row in range(1, N_ROW - 2, 2)] + ahead)
    upper_even = lax.ppermute(even, "row", [(row, row - 2) for row in range(3, N_ROW, 2)])
    outgoing, shares = call(
        rows_kernel,
        [(PARTS * 16, 128), (N_COL, 2, LOW, COLS)],
        (0, 1),
        pos,
        leds,
        own,
        lower_odd,
        upper_even,
        lower_even,
        upper_odd,
        twist,
        part_table,
        hbm=True,
        limit=ROWS_VMEM_BYTES,
    )(
        [
            pltpu.VMEM((N_COL, 2, LOW, COLS), F32),
            pltpu.VMEM((PARTS * 16, 128), F32),
            pltpu.VMEM((4, COLS, 128), F32),
            pltpu.SemaphoreType.DMA((N_COL + 1,)),
        ]
    )
    back_shares = [shares[0]] + [
        lax.ppermute(shares[step], "col", [(at, (at + step) % N_COL) for at in range(N_COL)])
        for step in range(1, N_COL)
    ]
    (total,) = call(assemble_kernel, [(2, ROWS, COLS)], (0,), pos, *back_shares)()
    incoming = lax.all_to_all(
        outgoing.reshape(PARTS, 16, 128), ("row", "col"), split_axis=0, concat_axis=0, tiled=True
    ).reshape(PARTS * 16, 128)
    (image,) = call(final_kernel, [(2, LOW, N)], (), incoming, twist, part_table, hbm=True)(
        [pltpu.VMEM((2, LOW, N), F32), pltpu.VMEM((2, COLS, PARTS), F32), pltpu.SemaphoreType.DMA((LOW // 8,))]
    )
    return (total, image)


def solution(mesh):
    window_table = dft_tables(M, 1.0 / math.sqrt(M))
    part_table = dft_tables(PARTS, 1.0 / math.sqrt(N))
    twist = twist_tables()
    mapped = jax.shard_map(
        on_device,
        mesh=mesh,
        in_specs=(
            P(None, "row", "col"),
            P(),
            P("row", "col", None, None),
            P("row", "col", None),
            P("row", "col"),
            P(),
            P(),
            P(),
        ),
        out_specs=(P(None, "row", "col"), P(None, ("row", "col"), None)),
        check_vma=False,
    )

    def run(spectrum, pupil, amplitude, offsets, holds):
        return mapped(
            spectrum,
            pupil,
            amplitude,
            offsets,
            holds,
            jnp.asarray(window_table),
            jnp.asarray(part_table),
            jnp.asarray(twist),
        )

    return run
```

```python
import math

import jax
import jax.numpy as jnp
import ml_dtypes
import numpy as np
from jax import lax
from jax.experimental import pallas as pl
from jax.experimental.pallas import tpu as pltpu
from jax.sharding import PartitionSpec as P

GAMMA = 1.0
N = 8192
M = 512
ROWS = 256
COLS = 1024
N_ROW = 32
N_COL = 8
PARTS = N_ROW * N_COL
LOW = 32
RING = 8
ORDER = [0, 2, 4, 6, 1, 3, 5, 7]
F32 = jnp.float32
BF16 = jnp.bfloat16
VMEM_BYTES = 32 * 1024 * 1024
SLOW = 10**11
ROWS_VMEM_BYTES = 59 * 1024 * 1024


def halves(table):
    high = table.astype(np.float32).astype(ml_dtypes.bfloat16)
    low = (table - high.astype(np.float64)).astype(np.float32).astype(ml_dtypes.bfloat16)
    return high, low


def dft_tables(length, scale):
    counter = np.arange(length)
    angles = 2.0 * np.pi / length * (np.outer(counter, counter) % length)
    return np.stack(halves(np.cos(angles) * scale) + halves(np.sin(angles) * scale))


def twist_tables():
    angles = 2.0 * np.pi / N * np.outer(np.arange(LOW), np.arange(PARTS))
    return np.stack([np.cos(angles), np.sin(angles)]).astype(np.float32)


def split(values):
    high = values.astype(BF16)
    low = (values - high.astype(F32)).astype(BF16)
    return high, low


def mm(left, right):
    return jnp.dot(left, right, preferred_element_type=F32)


def six(first, second, axis):
    return jnp.concatenate([first[0], first[1], first[0], second[0], second[1], second[0]], axis=axis)


def six_table(first, second, axis):
    return jnp.concatenate([first[0], first[0], first[1], second[0], second[0], second[1]], axis=axis)


def minus(pair):
    return -pair[0], -pair[1]


def complex_times_table(re, im, cos, sin, sign):
    first, second = (minus(im), re) if sign > 0 else (im, minus(re))
    return (
        mm(six(re, first, 1), six_table(cos, sin, 0)),
        mm(six(second, im, 1), six_table(sin, cos, 0)),
    )


def table_times_complex(cos, sin, sign, re, im):
    first, second = (minus(im), re) if sign > 0 else (im, minus(re))
    return (
        mm(six_table(cos, sin, 1), six(re, first, 0)),
        mm(six_table(sin, cos, 1), six(second, im, 0)),
    )


def turn(value, numer, denom):
    re, im = value
    numer %= denom
    if numer == 0:
        return re, im
    if 4 * numer == denom:
        return -im, re
    if 2 * numer == denom:
        return -re, -im
    cos = math.cos(2.0 * math.pi * numer / denom)
    sin = math.sin(2.0 * math.pi * numer / denom)
    if 8 * numer == denom:
        return (re - im) * cos, (re + im) * cos
    if 8 * numer == 3 * denom:
        return (re + im) * -sin, (re - im) * sin
    return re * cos - im * sin, re * sin + im * cos


def fft_list(values):
    count = len(values)
    if count == 1:
        return values
    even = fft_list(values[0::2])
    odd = fft_list(values[1::2])
    first, second = [], []
    for at in range(count // 2):
        er, ei = even[at]
        tr, ti = turn(odd[at], at, count)
        first.append((er + tr, ei + ti))
        second.append((er - tr, ei - ti))
    return first + second


def call(kernel, outs, smem, *args, cost=None, hbm=False, limit=VMEM_BYTES):
    specs = [pl.BlockSpec(memory_space=pltpu.SMEM if at in smem else pltpu.VMEM) for at in range(len(args))]
    return lambda scratch=(): pl.pallas_call(
        kernel,
        out_shape=tuple(jax.ShapeDtypeStruct(shape, F32) for shape in outs),
        in_specs=specs,
        out_specs=tuple(pl.BlockSpec(memory_space=pltpu.HBM if hbm else pltpu.VMEM) for _ in outs),
        scratch_shapes=scratch,
        cost_estimate=cost and pl.CostEstimate(flops=cost, bytes_accessed=0, transcendentals=0),
        compiler_params=pltpu.CompilerParams(vmem_limit_bytes=limit),
    )(*args)


def frame(pos, corner):
    return corner[0] - pos[0] * ROWS, corner[1] - pos[1] * COLS


def corners(pos, local, lower, upper):
    moved = jnp.logical_and(lax.rem(pos[0], 2) == 0, lax.rem(pos[1], 2) == 1)
    first = lax.rem(pos[0], RING) == 0
    local, lower, upper = frame(pos, local), frame(pos, lower), frame(pos, upper)
    shared = tuple(jnp.where(first, x, y) for x, y in zip(upper, lower))
    here = tuple(jnp.where(moved, x, y) for x, y in zip(shared, local))
    up = tuple(jnp.where(moved, x, y) for x, y in zip(local, upper))
    return here, lower, up


def inside(rows, start):
    return jnp.logical_and(rows >= start, rows < start + M)


def pack_kernel(pos, local, lower, upper, spec, to_lower, to_upper):
    _, down, up = corners(pos, local, lower, upper)
    cols = lax.broadcasted_iota(jnp.int32, (ROWS, M), 1)
    for part in range(2):
        left = spec[part, :, :M]
        right = spec[part, :, M:]
        to_lower[part] = jnp.where(cols >= down[1], left, right)
        to_upper[part] = jnp.where(cols >= up[1], left, right)


def pupil_kernel(pos, local, lower, upper, pupil, amplitude, near_amp, rolled, measured, far_half):
    (at_row, at_col), _, _ = corners(pos, local, lower, upper)
    shift = lax.rem(at_col, M)
    down = lax.rem(at_row + 2 * N, M)
    for part in range(2):
        rolled[part] = pltpu.roll(pltpu.roll(pupil[part], shift, 1), down, 0)[:ROWS]
    low = lax.rem(pos[0], 2) == 0
    moved = jnp.logical_and(low, lax.rem(pos[1], 2) == 1)
    own = jnp.where(low, amplitude[:, :ROWS], amplitude[:, ROWS:])
    measured[...] = jnp.where(moved, 0.0, own) + near_amp[...]
    far_half[...] = amplitude[:, :ROWS]


def stage_kernel(spec, staged):
    staged[...] = spec[...]


def half_rows(table, half):
    where = pl.ds(pl.multiple_of(half * ROWS, ROWS), ROWS)
    return (table[0, where, :], table[1, where, :]), (table[2, where, :], table[3, where, :])


def half_cols(table, half):
    where = pl.ds(pl.multiple_of(half * ROWS, ROWS), ROWS)
    return (table[0, :, where], table[1, :, where]), (table[2, :, where], table[3, :, where])


def field_of(where, spec, from_lower, from_upper, pupil):
    (at_row, at_col), _, _ = corners(*where)
    row, col = where[0][0], where[0][1]
    around = jnp.logical_and(lax.rem(row, RING) == 0, lax.rem(col, 2) == 1)
    ahead = jnp.where(around, RING * ROWS, M)
    cols = lax.broadcasted_iota(jnp.int32, (ROWS, M), 1)
    rows = lax.broadcasted_iota(jnp.int32, (ROWS, M), 0)
    field = []
    for part in range(2):
        own = jnp.where(cols >= at_col, spec[part, :, :M], spec[part, :, M:])
        other = jnp.where(inside(rows + ahead, at_row), from_upper[part], from_lower[part])
        field.append(jnp.where(inside(rows, at_row), own, other))
    re = split(pupil[0] * field[0] - pupil[1] * field[1])
    im = split(pupil[0] * field[1] + pupil[1] * field[0])
    return re, im


def send_kernel(pos, local, lower, upper, spec, from_lower, from_upper, pupil, table, send):
    re, im = field_of((pos, local, lower, upper), spec, from_lower, from_upper, pupil)
    cos, sin = half_cols(table, 1 - lax.rem(pos[0], 2))
    send[0], send[1] = complex_times_table(re, im, cos, sin, 1)


def keep_kernel(pos, local, lower, upper, spec, from_lower, from_upper, pupil, table, wave):
    parity = lax.rem(pos[0], 2)
    re, im = field_of((pos, local, lower, upper), spec, from_lower, from_upper, pupil)
    cos, sin = half_cols(table, parity)
    re, im = complex_times_table(re, im, cos, sin, 1)
    wave[0], wave[1] = table_times_complex(cos, sin, 1, split(re), split(im))


def fit_kernel(pos, far_amp, measured, wave, other, table, fit, send):
    parity = lax.rem(pos[0], 2)
    cos, sin = half_cols(table, 1 - parity)
    wave_re, wave_im = table_times_complex(cos, sin, 1, split(other[0]), split(other[1]))
    wave_re += wave[0]
    wave_im += wave[1]
    modulus = jnp.sqrt(wave_re * wave_re + wave_im * wave_im + GAMMA)
    keeping = 1.0 - (measured[...] + far_amp[...]) / modulus
    fit[0] = wave_re * keeping
    fit[1] = wave_im * keeping
    cos, sin = half_rows(table, 1 - parity)
    send[0], send[1] = table_times_complex(cos, sin, -1, split(fit[0]), split(fit[1]))


def stay_kernel(pos, fit, table, part):
    cos, sin = half_rows(table, lax.rem(pos[0], 2))
    re, im = table_times_complex(cos, sin, -1, split(fit[0]), split(fit[1]))
    part[0], part[1] = complex_times_table(split(re), split(im), cos, sin, -1)


def grad_kernel(pos, part, other, pupil, table, grad):
    cos, sin = half_rows(table, 1 - lax.rem(pos[0], 2))
    re, im = complex_times_table(split(other[0]), split(other[1]), cos, sin, -1)
    re += part[0]
    im += part[1]
    back_re = pupil[0] * re + pupil[1] * im
    back_im = pupil[0] * im - pupil[1] * re
    for at, col in enumerate(ORDER):
        grad[at, 0] = back_re[col * LOW : col * LOW + LOW]
        grad[at, 1] = back_im[col * LOW : col * LOW + LOW]


def rows_kernel(pos, leds, own, lower_odd, upper_even, lower_even, upper_odd, twist, table, outgoing, shares, pencil, spectra, digits, sems):
    row, col = pos[0], pos[1]
    cols = lax.broadcasted_iota(jnp.int32, (LOW, M), 1)
    rows = lax.broadcasted_iota(jnp.int32, (LOW, M), 0) + col * LOW
    for at, source_col in enumerate(ORDER):
        lower, upper = (lower_even, upper_even) if at < 4 else (lower_odd, upper_odd)
        corner = [leds[source_col, index] for index in range(6)]
        around = corners((row, source_col), corner[:2], corner[2:4], corner[4:])
        for part in range(2):
            left = right = 0.0
            for (at_row, at_col), source in zip(around, (own[at, part], lower[at % 4, part], upper[at % 4, part])):
                value = jnp.where(inside(rows, at_row), source, 0.0)
                left = left + jnp.where(cols >= at_col, value, 0.0)
                right = right + jnp.where(cols < at_col, value, 0.0)
            pencil[source_col, part, :, :M] = left
            pencil[source_col, part, :, M:] = right
    copies = [
        pltpu.make_async_copy(
            pencil.at[source_col], shares.at[lax.rem(source_col - col + N_COL, N_COL)], sems.at[source_col]
        )
        for source_col in range(N_COL)
    ]
    for copy in copies:
        copy.start()
    for group in range(LOW // 8):
        for tile in range(2):
            lanes = slice(tile * 128, tile * 128 + 128)
            values = [
                tuple(
                    pencil[
                        at // 4,
                        part,
                        group * 8 : group * 8 + 8,
                        (at % 4) * 256 + tile * 128 : (at % 4) * 256 + tile * 128 + 128,
                    ]
                    for part in range(2)
                )
                for at in range(LOW)
            ]
            for at, (re, im) in enumerate(fft_list(values)):
                cos = twist[0, at : at + 1, lanes]
                sin = twist[1, at : at + 1, lanes]
                place = pl.ds((at // 8) * 256 + group * 64 + at % 8, 8, 8)
                digits[tile, place, :] = re * cos - im * sin
                digits[2 + tile, place, :] = re * sin + im * cos
    re = split(jnp.concatenate([digits[0], digits[1]], axis=1))
    im = split(jnp.concatenate([digits[2], digits[3]], axis=1))
    cos = (table[0], table[1])
    sin = (table[2], table[3])
    for part, flat in enumerate(complex_times_table(re, im, cos, sin, 1)):
        turned = flat.T
        for at in range(8):
            spectra[pl.ds(part * 8 + at, PARTS, 16), :] = turned[:, at * 128 : at * 128 + 128]
    last = pltpu.make_async_copy(spectra, outgoing, sems.at[N_COL])
    last.start()
    for copy in copies:
        copy.wait()
    last.wait()


def assemble_kernel(pos, *refs):
    total = refs[-1]
    for step, share in enumerate(refs[:-1]):
        where = pl.ds(pl.multiple_of(lax.rem(pos[1] - step + N_COL, N_COL) * LOW, LOW), LOW)
        for part in range(2):
            total[part, where, :] = share[part]


def final_kernel(incoming, twist, table, result, image, digits, sems):
    pair = []
    for part in range(2):
        flat = jnp.concatenate([incoming[pl.ds(part * 8 + at, PARTS, 16), :] for at in range(8)], axis=1)
        pair.append(split(flat.T))
    cos = (table[0], table[1])
    sin = (table[2], table[3])
    digits[0], digits[1] = complex_times_table(*pair, cos, sin, 1)
    copies = []
    for group in range(LOW // 8):
        for tile in range(2):
            lanes = slice(tile * 128, tile * 128 + 128)
            values = []
            for at in range(LOW):
                rows = slice(group * 256 + at * 8, group * 256 + at * 8 + 8)
                re = digits[0, rows, lanes]
                im = digits[1, rows, lanes]
                cos = twist[0, at : at + 1, lanes]
                sin = twist[1, at : at + 1, lanes]
                values.append((re * cos - im * sin, re * sin + im * cos))
            for at, value in enumerate(fft_list(values)):
                for part in range(2):
                    image[
                        part,
                        group * 8 : group * 8 + 8,
                        at * 256 + tile * 128 : at * 256 + tile * 128 + 128,
                    ] = value[part]
        rows = pl.ds(group * 8, 8)
        copies.append(pltpu.make_async_copy(image.at[:, rows], result.at[:, rows], sems.at[group]))
        copies[-1].start()
    for copy in copies:
        copy.wait()


def moves(rule):
    pairs = [(row, col, rule(row, col % 2)) for row in range(N_ROW) for col in range(N_COL)]
    return [(row * N_COL + col, to * N_COL + col) for row, col, to in pairs if to is not None]


def downward(row, core):
    if row % RING == 0 and core == 1:
        return (row - RING) % N_ROW
    return (row - 2) % N_ROW if row % 2 == 1 or core == 0 else None


def second(row):
    return row + 2 if row % RING < RING - 2 else row - (RING - 2)


def upward(row, core):
    if row % 2 == 0:
        return second(row) if core == 1 else None
    return (row + 2) % N_ROW


def ring_step(row, by):
    return row // RING * RING + (row + by) % RING


def partner(row, core):
    return row ^ 1 if core == 0 else ring_step(row, 1 if row % 2 == 1 else -1)


def near(row, core):
    return row ^ 1 if core == 0 else ring_step(row, 1)


def far(row, core):
    return second(row) if core == 1 and row % 2 == 0 else None


def from_upper_row(row, core):
    return second(row) if core == 1 and row % 2 == 0 else (row - 2) % N_ROW


BOTH = ("row", "col")
DOWN = moves(downward)
UP = moves(upward)
PARTNERS = moves(partner)
NEAR = moves(near)
FAR = moves(far)
FROM_LOWER = moves(lambda row, core: (row + 2) % N_ROW)
FROM_UPPER = moves(from_upper_row)


def on_device(spectrum, pupil, amplitude, offsets, holds, window_table, part_table, twist):
    row = lax.axis_index("row")
    col = lax.axis_index("col")
    pos = jnp.stack([row, col]).astype(jnp.int32)
    local = offsets[0, 0]
    lower = lax.ppermute(local, BOTH, FROM_LOWER)
    upper = lax.ppermute(local, BOTH, FROM_UPPER)
    where = (pos, local, lower, upper)
    leds = lax.all_gather(jnp.concatenate([local, lower, upper]), "col")
    smem = (0, 1, 2, 3)
    measured = amplitude[0, 0]
    half = (ROWS, M)
    quarter = (2, ROWS, ROWS)
    near_half = lax.dynamic_slice(measured, (jnp.int32(0), (1 - row % 2) * ROWS), (M, ROWS))
    near_amp = lax.ppermute(near_half, BOTH, NEAR)

    (staged,) = call(stage_kernel, [(2, ROWS, COLS)], (), spectrum, limit=4 * 1024 * 1024)()
    to_lower, to_upper = call(pack_kernel, [(2,) + half, (2,) + half], smem, *where, staged, cost=SLOW, limit=4 * 1024 * 1024)()
    from_upper = lax.ppermute(to_lower, BOTH, DOWN)
    from_lower = lax.ppermute(to_upper, BOTH, UP)
    rolled, measured, far_half = call(
        pupil_kernel, [(2,) + half, (M, ROWS), (M, ROWS)], smem, *where, pupil, measured, near_amp, cost=SLOW
    )()
    far_amp = lax.ppermute(far_half, BOTH, FAR)

    sources = (*where, staged, from_lower, from_upper, rolled, window_table)
    (send,) = call(send_kernel, [quarter], smem, *sources)()
    other = lax.ppermute(send, BOTH, PARTNERS)
    (wave,) = call(keep_kernel, [(2, M, ROWS)], smem, *sources)()
    fit, send = call(
        fit_kernel, [(2, M, ROWS), quarter], (0,), pos, far_amp, measured, wave, other, window_table
    )()
    other = lax.ppermute(send, BOTH, PARTNERS)
    (part,) = call(stay_kernel, [(2,) + half], (0,), pos, fit, window_table)()
    (grad,) = call(grad_kernel, [(N_COL, 2, LOW, M)], (0,), pos, part, other, rolled, window_table)()

    own = lax.all_to_all(grad, "col", split_axis=0, concat_axis=0, tiled=True, axis_index_groups=[ORDER])
    even, odd = own[:4], own[4:]
    lower_even = lax.ppermute(even, "row", [(row, (row + 2) % N_ROW) for row in range(N_ROW)])
    upper_odd = lax.ppermute(odd, "row", [(row, row + RING - 2 if row % RING == 0 else (row - 2) % N_ROW) for row in range(N_ROW)])
    ahead = [(row, (row + RING) % N_ROW) for row in range(0, N_ROW, RING)]
    lower_odd = lax.ppermute(odd, "row", [(row, (row + 2) % N_ROW) for row in range(1, N_ROW, 2)] + ahead)
    upper_even = lax.ppermute(even, "row", [(row, (row - 2) % N_ROW) for row in range(1, N_ROW, 2)])
    outgoing, shares = call(
        rows_kernel,
        [(PARTS * 16, 128), (N_COL, 2, LOW, COLS)],
        (0, 1),
        pos,
        leds,
        own,
        lower_odd,
        upper_even,
        lower_even,
        upper_odd,
        twist,
        part_table,
        hbm=True,
        limit=ROWS_VMEM_BYTES,
    )(
        [
            pltpu.VMEM((N_COL, 2, LOW, COLS), F32),
            pltpu.VMEM((PARTS * 16, 128), F32),
            pltpu.VMEM((4, COLS, 128), F32),
            pltpu.SemaphoreType.DMA((N_COL + 1,)),
        ]
    )
    back_shares = [shares[0]] + [
        lax.ppermute(shares[step], "col", [(at, (at + step) % N_COL) for at in range(N_COL)])
        for step in range(1, N_COL)
    ]
    (total,) = call(assemble_kernel, [(2, ROWS, COLS)], (0,), pos, *back_shares)()
    incoming = lax.all_to_all(
        outgoing.reshape(PARTS, 16, 128), ("row", "col"), split_axis=0, concat_axis=0, tiled=True
    ).reshape(PARTS * 16, 128)
    (image,) = call(final_kernel, [(2, LOW, N)], (), incoming, twist, part_table, hbm=True)(
        [pltpu.VMEM((2, LOW, N), F32), pltpu.VMEM((2, COLS, PARTS), F32), pltpu.SemaphoreType.DMA((LOW // 8,))]
    )
    return (total, image)


def solution(mesh):
    window_table = dft_tables(M, 1.0 / math.sqrt(M))
    part_table = dft_tables(PARTS, 1.0 / math.sqrt(N))
    twist = twist_tables()
    mapped = jax.shard_map(
        on_device,
        mesh=mesh,
        in_specs=(
            P(None, "row", "col"),
            P(),
            P("row", "col", None, None),
            P("row", "col", None),
            P("row", "col"),
            P(),
            P(),
            P(),
        ),
        out_specs=(P(None, "row", "col"), P(None, ("row", "col"), None)),
        check_vma=False,
    )

    def run(spectrum, pupil, amplitude, offsets, holds):
        return mapped(
            spectrum,
            pupil,
            amplitude,
            offsets,
            holds,
            jnp.asarray(window_table),
            jnp.asarray(part_table),
            jnp.asarray(twist),
        )

    return run
```
